128 devices in a mesh: obj: 16 (over y, z), pat: 8 (over x, core).
Axes of the slice: x: 4, y: 4, z: 4, core: 2. Of those that a mesh axis runs over, the one named last changes fastest.
Arguments:
- object_field: float32 [2, 2048, 2048], P(None, 'obj', 'pat'), may hold values from -6 to 6
- probe: float32 [2, 512, 512], replicated, may hold values from -5 to 5
- scan_cols: int32 [256], P(('obj', 'pat')), may hold values from -1 to 24, as said below
- amplitudes: float32 [256, 512, 512], P(('obj', 'pat')), may hold values from 0.05 to 3
Outputs:
- object_next: float32 [2, 2048, 2048], P(None, 'obj', 'pat')
- probe_next: float32 [2, 512, 512], replicated
The draws below stay inside these ranges and needn't reach their ends.
Inputs may be any that keep to these rules, and one draw needn't show every extreme that they name: `scan_cols`: the first slot of every worker is filled; within a band group the filled slots name distinct columns; every band group has a slot at column 24.
All inputs are finite; a program needn't handle non-finite values.
Results may differ from the reference program's by a relative error of at most 0.015.
Values sent between devices are 32-bit elements; how exact they have to be, the bound alone decides.
A program may use at most 128 MiB of HBM per device.

```python
import math
import jax
import jax.numpy as jnp
from jax import lax

N = 512
ITERS = 2
SLOTS = 2
RB = 128
NR = 2048
NC = 2048
POSITIONS = 256
N_OBJ = 16
N_PAT = 8


def draw_scan_cols(key, part):
    key = jax.random.fold_in(key, 5)
    places = 4 * N_PAT - 7
    per_group = N_PAT * SLOTS
    slot_index = jnp.arange(per_group, dtype=jnp.int32)

    def one_group(group):
        group_key = jax.random.fold_in(key, group)
        key_perm, key_most, key_empty, key_drop = jax.random.split(group_key, 4)
        others = jax.random.permutation(key_perm, places - 1).astype(jnp.int32)
        most_worker = jax.random.randint(key_most, (), 0, N_PAT)
        empty_worker = (most_worker + 1 + jax.random.randint(key_empty, (), 0, N_PAT - 1)) % N_PAT
        most_slot = most_worker * SLOTS
        shifted = slot_index - (slot_index > most_slot).astype(jnp.int32)
        shifted = jnp.clip(shifted, 0, places - 2)
        values = jnp.where(slot_index == most_slot, places - 1, others[shifted])
        drop = jax.random.randint(key_drop, (per_group,), 0, 3) == 0
        forced = slot_index == empty_worker * SLOTS + SLOTS - 1
        empty = (slot_index % SLOTS > 0) & (drop | forced)
        return jnp.where(empty, -1, values).astype(jnp.int32)
    groups = jnp.arange(N_OBJ, dtype=jnp.int32)
    return jax.vmap(one_group)(groups).reshape(-1).astype(jnp.int32)


def shard_levels(key, shape, shards, least, high):
    level = 1.0
    for dim, blocks in shards:
        steps = jax.random.uniform(jax.random.fold_in(jax.random.fold_in(key, 6), dim), (blocks,), jnp.float32, least / len(shards), high / len(shards))
        level = level * jnp.repeat(jnp.exp(steps), shape[dim] // blocks).reshape((-1,) + (1,) * (len(shape) - 1 - dim))
    return level


def normal_values(rng, extent, width, reach, cuts=(), kind=jnp.bfloat16):
    loudness = shard_levels(rng, extent, cuts, -0.22, 0.18) if cuts else 1.0
    values = jax.random.normal(rng, extent, jnp.float32) * width * loudness
    return jnp.minimum(jnp.maximum(values, -reach), reach).astype(kind)


def setup_inputs(seed: int = 0) -> dict:
    key_of = jax.random.split(jax.random.key(seed), 5)
    object_field = normal_values(key_of[0], (2, NR, NC), 1.0, 6.0, ((1, 16), (2, 8)), jnp.float32)
    probe = normal_values(key_of[1], (2, N, N), 0.7, 5.0, (), jnp.float32)
    scan_cols = draw_scan_cols(jax.random.fold_in(key_of[4], 71), 0)
    amplitudes = jnp.clip(jnp.exp(math.log(3.0) - 4.0943445 * jax.random.uniform(key_of[3], (POSITIONS, N, N), jnp.float32) ** shard_levels(key_of[3], (POSITIONS, N, N), ((0, 128),), -0.2, 0.2)), 0.05, 3.0)
    return dict(object_field=object_field, probe=probe, scan_cols=scan_cols, amplitudes=amplitudes)


def make_tables(size):
    index = jnp.arange(size, dtype=jnp.int32)
    product = index[:, None] * index[None, :] % size
    angle = product.astype(jnp.float32) * jnp.float32(2.0 * math.pi / size)
    scale = jnp.float32(1.0 / math.sqrt(size))
    real_part = jnp.cos(angle) * scale
    imag_part = -jnp.sin(angle) * scale
    fwd_left = jnp.concatenate([jnp.concatenate([real_part, -imag_part], 1), jnp.concatenate([imag_part, real_part], 1)], 0)
    fwd_right = jnp.concatenate([jnp.concatenate([real_part, imag_part], 1), jnp.concatenate([-imag_part, real_part], 1)], 0)
    return (fwd_left.astype(jnp.bfloat16), fwd_right.astype(jnp.bfloat16))

def transform(real_in, imag_in, left, right):
    size = real_in.shape[0]
    stacked = jnp.concatenate([real_in, imag_in], 0).astype(jnp.bfloat16)
    middle = jnp.dot(left, stacked, preferred_element_type=jnp.float32).astype(jnp.bfloat16)
    beside = jnp.concatenate([middle[:size], middle[size:]], 1)
    result = jnp.dot(beside, right, preferred_element_type=jnp.float32)
    return (result[:, :size], result[:, size:])

def exit_update(patch, probe, amplitude, valid, fwd_left, fwd_right):
    probe_re, probe_im = (probe[0], probe[1])
    patch_re, patch_im = (patch[0], patch[1])
    psi_re = probe_re * patch_re - probe_im * patch_im
    psi_im = probe_re * patch_im + probe_im * patch_re
    wave_re, wave_im = transform(psi_re, psi_im, fwd_left, fwd_right)
    magnitude = jnp.sqrt(wave_re * wave_re + wave_im * wave_im)
    factor = amplitude / jnp.maximum(magnitude, 0.25)
    back_re, back_im = transform(wave_re * factor, wave_im * factor, fwd_right, fwd_left)
    diff_re = (back_re - psi_re) * valid
    diff_im = (back_im - psi_im) * valid
    object_part = jnp.stack([probe_re * diff_re + probe_im * diff_im, probe_re * diff_im - probe_im * diff_re])
    probe_part = jnp.stack([patch_re * diff_re + patch_im * diff_im, patch_re * diff_im - patch_im * diff_re])
    return (object_part, probe_part)

def reference(object_field, probe, scan_cols, amplitudes):
    fwd_left, fwd_right = make_tables(N)
    total = N_OBJ * N_PAT * SLOTS
    indices = jnp.arange(total, dtype=jnp.int32)
    valid_all = (scan_cols >= 0).astype(jnp.float32)
    count = jnp.sum(valid_all)
    for step in range(ITERS):
        padded = jnp.pad(object_field, ((0, 0), (0, 3 * RB), (0, 0)))

        def one_slot(carry, inputs):
            grad, probe_grad = carry
            column, amplitude, index, valid = inputs
            group = index // SLOTS // N_PAT
            row_start = (group * RB).astype(jnp.int32)
            col_start = (jnp.maximum(column, 0) * (N // 8)).astype(jnp.int32)
            zero = jnp.int32(0)
            patch = lax.dynamic_slice(padded, (zero, row_start, col_start), (2, N, N))
            object_part, probe_part = exit_update(patch, probe, amplitude, valid, fwd_left, fwd_right)
            region = lax.dynamic_slice(grad, (zero, row_start, col_start), (2, N, N))
            grad = lax.dynamic_update_slice(grad, region + object_part, (zero, row_start, col_start))
            return ((grad, probe_grad + probe_part), None)
        start_grad = jnp.zeros(padded.shape, jnp.float32)
        start_probe = jnp.zeros(probe.shape, jnp.float32)
        (grad, probe_grad), unused = lax.scan(one_slot, (start_grad, start_probe), (scan_cols, amplitudes, indices, valid_all))
        object_field = object_field + 0.25 * grad[:, :NR]
        probe = probe + probe_grad / count
    return (object_field, probe)
```

```python
import functools
import math

import jax
import jax.numpy as jnp
import ml_dtypes
import numpy as np
from jax import lax
from jax.experimental import pallas as pl
from jax.experimental.pallas import tpu as pltpu
from jax.sharding import PartitionSpec as P

N = 512
RB = 128
SLOTS = 2
TILES = 16
MESH = pl.DeviceIdType.MESH
F32 = jnp.float32
BF16 = jnp.bfloat16


def tables():
    index = np.arange(N)
    angle = (index[:, None] * index[None, :] % N) * (2.0 * math.pi / N)
    real = np.cos(angle) / math.sqrt(N)
    imag = -np.sin(angle) / math.sqrt(N)
    left = np.block([[real, -imag], [imag, real]])
    right = np.block([[real, imag], [-imag, real]])
    return left.astype(ml_dtypes.bfloat16), right.astype(ml_dtypes.bfloat16)


def place():
    o = lax.axis_index("obj")
    p = lax.axis_index("pat")
    return o // 4, lax.rem(o, 4), p // 2, lax.rem(p, 2)


def ring(value, step):
    return lax.rem(value + (step + 4), 4)


class Links:
    def __init__(self, send_sems, recv_sems):
        self.send_sems, self.recv_sems, self.used, self.copies = send_sems, recv_sems, 0, []
        self.y, self.z, self.x, self.c = place()

    def target(self, dy=0, dz=0, dx=0, dc=0):
        core = self.c if dc == 0 else 1 - self.c
        return (ring(self.y, dy) * 4 + ring(self.z, dz), ring(self.x, dx) * 2 + core)

    def send(self, src, dst, device):
        k = self.used
        self.used += 1
        copy = pltpu.make_async_remote_copy(
            src_ref=src, dst_ref=dst, send_sem=self.send_sems.at[k], recv_sem=self.recv_sems.at[k],
            device_id=device, device_id_type=MESH,
        )
        copy.start()
        self.copies.append(copy)
        return copy

    def group(self, step):
        o = lax.axis_index("obj")
        return (lax.rem(o + (step + 16), 16), lax.axis_index("pat"))

    def drain(self):
        for copy in self.copies:
            copy.wait_send()


def greet(devices):
    barrier = pltpu.get_barrier_semaphore()
    for device in devices:
        pl.semaphore_signal(barrier, inc=1, device_id=device, device_id_type=MESH)
    pl.semaphore_wait(barrier, len(devices))


def band_at(band, pat, b, half=None):
    if half is None:
        return band.at[pl.ds(2 * pat, 2), :, pl.ds(b * RB, RB), :]
    return band.at[pl.ds(2 * pat + half, 1), :, pl.ds(b * RB, RB), :]


def gather_steps(links, tile, band, local_sem):
    x, c = links.x, links.c
    me = 2 * x + c
    sib = links.target(dc=1)
    up, down = links.target(dx=1), links.target(dx=-1)
    before, after, across = 2 * ring(x, -1) + c, 2 * ring(x, 1) + c, 2 * ring(x, 2) + c
    state = {}

    def start():
        own = pltpu.make_async_copy(tile, band_at(band, me, 0), local_sem)
        own.start()
        state["own"] = own
        state["yz"] = {b: links.send(tile, band_at(band, me, b), links.group(-b)) for b in (1, 2, 3)}

    def first(b):
        src = tile
        if b:
            state["yz"][b].wait_recv()
            src = band_at(band, me, b)
        dst = band_at(band, me, b)
        state["up", b] = links.send(src, dst, up)
        state["down", b] = links.send(src, dst, down)
        state["sib", b] = [links.send(src, dst, sib)]

    def second(b):
        state["up", b].wait_recv()
        half, whole = band_at(band, before, b, 0), band_at(band, before, b)
        state["up2", b] = links.send(half, half, up)
        state["sib", b].append(links.send(whole, whole, sib))
        state["down", b].wait_recv()
        half, whole = band_at(band, after, b, 1), band_at(band, after, b)
        state["down2", b] = links.send(half, half, down)
        state["sib", b].append(links.send(whole, whole, sib))

    def third(b):
        state["up2", b].wait_recv()
        state["down2", b].wait_recv()
        whole = band_at(band, across, b)
        state["sib", b].append(links.send(whole, whole, sib))

    def finish():
        state["own"].wait()
        for b in range(4):
            for copy in state["sib", b]:
                copy.wait_recv()

    order = [start]
    for kind, b in ((first, 0), (first, 1), (second, 0), (first, 2), (second, 1), (third, 0), (first, 3),
                    (second, 2), (third, 1), (second, 3), (third, 2), (third, 3)):
        order.append(functools.partial(kind, b))
    return order + [finish]


GATHER_SENDS = 3 + 4 * 8


def gather_kernel(tile, band, send_sems, recv_sems, local_sem):
    links = Links(send_sems, recv_sems)
    groups = [links.group(s) for s in (-3, -2, -1, 1, 2, 3)]
    greet(groups + [links.target(dx=1), links.target(dx=-1), links.target(dc=1)])
    for step in gather_steps(links, tile, band, local_sem):
        step()
    links.drain()


def reduce_steps(links, grad, tile_in, tile_out, bufs, local_sems):
    own, sibs, halves, wholes, rows = bufs
    x, c = links.x, links.c
    o = lax.axis_index("obj")
    sib = links.target(dc=1)
    up, down = links.target(dx=1), links.target(dx=-1)
    before, after, across = ring(x, -1), ring(x, 1), ring(x, 2)
    state = {}

    def start():
        for b in (3, 2, 1, 0):
            mine = grad.at[:, c, :, :, pl.ds(b * RB, RB), :]
            theirs = grad.at[:, 1 - c, :, :, pl.ds(b * RB, RB), :]
            state["sib", b] = links.send(theirs, sibs.at[b], sib)
            copy = pltpu.make_async_copy(mine, own.at[b], local_sems.at[b])
            copy.start()
            state["own", b] = copy

    def first(b):
        state["own", b].wait()
        state["sib", b].wait_recv()

        @pl.loop(0, 4)
        def _(k):
            own[b, k] = own[b, k] + sibs[b, k]

        state["up", b] = links.send(own.at[b, across, 0], halves.at[b, 0], up)
        state["down", b] = links.send(own.at[b, across, 1], halves.at[b, 1], down)

    def second(b):
        state["up", b].wait_recv()
        own[b, after, 0] = own[b, after, 0] + halves[b, 0]
        state["up2", b] = links.send(own.at[b, after], wholes.at[b, 0], up)
        state["down", b].wait_recv()
        own[b, before, 1] = own[b, before, 1] + halves[b, 1]
        state["down2", b] = links.send(own.at[b, before], wholes.at[b, 1], down)

    def third(b):
        state["up2", b].wait_recv()
        state["down2", b].wait_recv()
        own[b, x] = own[b, x] + (wholes[b, 0] + wholes[b, 1])
        if b:
            state["rows", b] = links.send(own.at[b, x], rows.at[b - 1], links.group(b))

    def finish():
        total = own[0, x]
        for b in (1, 2, 3):
            state["rows", b].wait_recv()
            total = total + jnp.where(o >= b, rows[b - 1], 0.0)
        tile_out[...] = tile_in[...] + 0.25 * total

    order = [start]
    for kind, b in ((first, 3), (first, 2), (second, 3), (first, 1), (second, 2), (third, 3), (first, 0),
                    (second, 1), (third, 2), (second, 0), (third, 1), (third, 0)):
        order.append(functools.partial(kind, b))
    return order + [finish]


REDUCE_SENDS = 4 * 5 + 3


def probe_steps(links, part, probe, count_in, probe_out, bufs, local_sems):
    q, q_sib, q_y, sum_y, q_z, sum_z, q_x, fresh, counts, got = bufs
    y, z, x, c = links.y, links.z, links.x, links.c
    sib = links.target(dc=1)
    state = {}

    def pull(key, n):
        for copy in state.pop(key):
            copy.wait_recv()
        total = counts[n]
        for k in range(1 if n == 0 else 3):
            total = total + got[n, k]
        counts[n + 1] = total

    def start():
        state["s"] = [links.send(part.at[1 - c], q_sib, sib), links.send(count_in, got.at[0, 0], sib)]
        copy = pltpu.make_async_copy(part.at[c], q, local_sems.at[0])
        copy.start()
        state["q"] = copy
        counts[0] = count_in[...]

    def over_y():
        state["q"].wait()
        pull("s", 0)

        @pl.loop(0, 4)
        def _(k):
            rows = pl.ds(k * 128, 128)
            q[rows, :] = q[rows, :] + q_sib[rows, :]

        state["y"] = []
        for k in (1, 2, 3):
            dev = links.target(dy=k)
            state["y"].append(links.send(q.at[pl.ds(128 * ring(y, k), 128), :], q_y.at[k - 1], dev))
            state["y"].append(links.send(counts.at[1], got.at[1, k - 1], dev))

    def over_z():
        pull("y", 1)
        sum_y[...] = q[pl.ds(128 * y, 128), :] + q_y[0] + q_y[1] + q_y[2]
        state["z"] = []
        for k in (1, 2, 3):
            dev = links.target(dz=k)
            state["z"].append(links.send(sum_y.at[pl.ds(32 * ring(z, k), 32), :], q_z.at[k - 1], dev))
            state["z"].append(links.send(counts.at[2], got.at[2, k - 1], dev))

    def over_x():
        pull("z", 2)
        sum_z[...] = sum_y[pl.ds(32 * z, 32), :] + q_z[0] + q_z[1] + q_z[2]
        state["x"] = []
        for k in (1, 2, 3):
            dev = links.target(dx=k)
            state["x"].append(links.send(sum_z.at[pl.ds(8 * ring(x, k), 8), :], q_x.at[k - 1], dev))
            state["x"].append(links.send(counts.at[3], got.at[3, k - 1], dev))

    def back_x():
        pull("x", 3)
        row = 128 * y + 32 * z + 8 * x
        total = sum_z[pl.ds(8 * x, 8), :] + q_x[0] + q_x[1] + q_x[2]
        count = counts[4][:, :1]
        fresh[...] = probe[c, pl.ds(row, 8), :] + total / count
        spot = probe_out.at[c, pl.ds(row, 8), :]
        copy = pltpu.make_async_copy(fresh, spot, local_sems.at[1])
        copy.start()
        state["fresh"] = copy
        state["bx"] = [links.send(fresh, spot, links.target(dx=k)) for k in (1, 2, 3)]

    def back_z():
        state["fresh"].wait()
        for copy in state.pop("bx"):
            copy.wait_recv()
        spot = probe_out.at[c, pl.ds(128 * y + 32 * z, 32), :]
        state["bz"] = [links.send(spot, spot, links.target(dz=k)) for k in (1, 2, 3)]

    def back_y():
        for copy in state.pop("bz"):
            copy.wait_recv()
        spot = probe_out.at[c, pl.ds(128 * y, 128), :]
        state["by"] = [links.send(spot, spot, links.target(dy=k)) for k in (1, 2, 3)]

    def back_sib():
        for copy in state.pop("by"):
            copy.wait_recv()
        spot = probe_out.at[c]
        state["bs"] = links.send(spot, spot, sib)

    def finish():
        state["bs"].wait_recv()

    return [start, over_y, over_z, over_x, back_x, back_z, back_y, back_sib, finish]


PROBE_SENDS = 2 + 18 + 9 + 1


def step_kernel(gather, grad, part, tile_in, probe, count_in, *refs):
    refs = list(refs)
    tile_out, probe_out = refs[:2]
    refs = refs[2:]
    band = refs.pop(0) if gather else None
    reduce_bufs, refs = refs[:5], refs[5:]
    probe_bufs, refs = refs[:10], refs[10:]
    send_sems, recv_sems, local_sems = refs
    links = Links(send_sems, recv_sems)
    groups = [links.group(s) for s in (-3, -2, -1, 1, 2, 3)]
    far = [links.target(dy=k) for k in (1, 2, 3)] + [links.target(dz=k) for k in (1, 2, 3)]
    near = [links.target(dx=k) for k in (1, 2, 3)] + [links.target(dc=1)]
    greet(groups + far + near)
    reduce = reduce_steps(links, grad, tile_in, tile_out, reduce_bufs, local_sems)
    probes = probe_steps(links, part, probe, count_in, probe_out, probe_bufs, local_sems.at[pl.ds(4, 2)])
    order = reduce[:1] + probes[:1] + reduce[1:3] + probes[1:2] + reduce[3:6] + probes[2:3] + reduce[6:8] + probes[3:4]
    order += reduce[8:10] + probes[4:5] + reduce[10:11] + probes[5:6] + reduce[11:12] + probes[6:7] + reduce[12:]
    if gather:
        more = gather_steps(links, tile_out, band, local_sems.at[6])
        order += more[:6] + probes[7:8] + more[6:] + probes[8:]
    else:
        order += probes[7:]
    for step in order:
        step()
    links.drain()


def compute_kernel(cols, band, probe, amps, left, right, grad, probe_grad,
                   win, patch, prb, amp, lt, rt, xs, ws, yr, yi, gsum, sems):
    o = lax.axis_index("obj")

    def window(s):
        first = jnp.minimum(jnp.maximum(cols[s], 0) // 2, 11)
        return pltpu.make_async_copy(band.at[pl.ds(first, 5)], win.at[s], sems.at[s])

    loads = [
        pltpu.make_async_copy(probe, prb, sems.at[2]),
        pltpu.make_async_copy(left, lt, sems.at[3]),
        pltpu.make_async_copy(right, rt, sems.at[4]),
        pltpu.make_async_copy(amps, amp, sems.at[5]),
    ]
    window(0).start()
    for load in loads:
        load.start()
    window(1).start()

    @pl.loop(0, TILES + 1)
    def _(t):
        gsum[t] = jnp.zeros((2, N, 128), F32)

    lane = lax.broadcasted_iota(jnp.int32, (32, 128), 1)

    def product(lhs, rhs):
        return jnp.dot(lhs, rhs, preferred_element_type=F32)

    def left_pass(table):
        for n in range(2):
            cut = slice(256 * n, 256 * n + 256)
            mid = product(table[...], xs[:, cut]).astype(BF16)
            ws[:, cut] = mid[:N]
            ws[:, 512 + 256 * n:768 + 256 * n] = mid[N:]

    def right_pass(table):
        for n in range(2):
            cut = slice(256 * n, 256 * n + 256)
            yr[:, cut] = product(ws[...], table[:, cut])
            yi[:, cut] = product(ws[...], table[:, 512 + 256 * n:768 + 256 * n])

    def slot(s, carry):
        col = cols[s]
        place_col = jnp.maximum(col, 0)
        valid = (col >= 0).astype(F32)
        first = jnp.minimum(place_col // 2, 11)
        shift = place_col // 2 - first
        odd = lax.rem(place_col, 2) == 1
        window(s).wait()

        @pl.when(s == 0)
        def _():
            loads[0].wait()

        @pl.loop(0, 16)
        def _(m):
            rows = pl.ds(pl.multiple_of(m * 32, 32), 32)
            inside = o * RB + m * 32 < TILES * RB
            for j in range(4):
                cut = slice(128 * j, 128 * j + 128)
                near, far = j + shift, jnp.minimum(j + shift + 1, 4)
                value = []
                for part in range(2):
                    a, b = win[s, near, part, rows, :], win[s, far, part, rows, :]
                    moved = jnp.where(lane < 64, pltpu.roll(a, 64, 1), pltpu.roll(b, 64, 1))
                    v = jnp.where(inside, jnp.where(odd, moved, a), 0.0)
                    patch[part, rows, cut] = v
                    value.append(v)
                re, im = value
                pre, pim = prb[0, rows, cut], prb[1, rows, cut]
                xs[rows, cut] = (pre * re - pim * im).astype(BF16)
                xs[pl.ds(pl.multiple_of(512 + m * 32, 32), 32), cut] = (pre * im + pim * re).astype(BF16)

        @pl.when(s == 0)
        def _():
            loads[1].wait()
            loads[2].wait()

        left_pass(lt)
        right_pass(rt)

        @pl.when(s == 0)
        def _():
            loads[3].wait()

        @pl.loop(0, 16)
        def _(m):
            rows = pl.ds(pl.multiple_of(m * 32, 32), 32)
            re, im = yr[rows, :], yi[rows, :]
            factor = amp[s, rows, :] * lax.rsqrt(jnp.maximum(re * re + im * im, 0.0625))
            xs[rows, :] = (re * factor).astype(BF16)
            xs[pl.ds(pl.multiple_of(512 + m * 32, 32), 32), :] = (im * factor).astype(BF16)

        left_pass(rt)
        right_pass(lt)
        first_out = first + shift

        @pl.loop(0, 16)
        def _(m):
            rows = pl.ds(pl.multiple_of(m * 32, 32), 32)
            last = [jnp.zeros((32, 128), F32)] * 2
            for j in range(5):
                if j < 4:
                    cut = slice(128 * j, 128 * j + 128)
                    re, im = patch[0, rows, cut], patch[1, rows, cut]
                    pre, pim = prb[0, rows, cut], prb[1, rows, cut]
                    dre = (yr[rows, cut] - (pre * re - pim * im)) * valid
                    dim = (yi[rows, cut] - (pre * im + pim * re)) * valid
                    gre, gim = re * dre + im * dim, re * dim - im * dre
                    keep = s == 0
                    probe_grad[0, rows, cut] = jnp.where(keep, gre, probe_grad[0, rows, cut] + gre)
                    probe_grad[1, rows, cut] = jnp.where(keep, gim, probe_grad[1, rows, cut] + gim)
                    parts = [pre * dre + pim * dim, pre * dim - pim * dre]
                else:
                    parts = [jnp.zeros((32, 128), F32)] * 2
                for part in range(2):
                    turned = pltpu.roll(parts[part], 64, 1) if j < 4 else parts[part]
                    moved = jnp.where(lane < 64, last[part], turned)
                    last[part] = turned
                    t = first_out + j
                    gsum[t, part, rows, :] = gsum[t, part, rows, :] + jnp.where(odd, moved, parts[part])

        return carry

    lax.fori_loop(0, SLOTS, slot, 0)
    out = pltpu.make_async_copy(gsum.at[pl.ds(0, TILES)], grad, sems.at[6])
    out.start()
    out.wait()


ANY = pl.BlockSpec(memory_space=pl.ANY)
VMEM = pl.BlockSpec(memory_space=pltpu.VMEM)
SMEM = pl.BlockSpec(memory_space=pltpu.SMEM)
TILE = (2, 2, RB, 128)
BAND = (TILES, 2, N, 128)


def f32(*shape):
    return pltpu.VMEM(shape, F32)


def params(collective_id=None):
    if collective_id is None:
        return pltpu.CompilerParams(vmem_limit_bytes=56 << 20)
    return pltpu.CompilerParams(vmem_limit_bytes=56 << 20, collective_id=collective_id, has_side_effects=True)


def gather_call(tile):
    return pl.pallas_call(
        gather_kernel,
        name="gather_band",
        out_shape=jax.ShapeDtypeStruct(BAND, F32),
        in_specs=[VMEM],
        out_specs=ANY,
        scratch_shapes=[pltpu.SemaphoreType.DMA((GATHER_SENDS,))] * 2 + [pltpu.SemaphoreType.DMA],
        compiler_params=params(1),
    )(tile)


def compute_call(cols, band, probe, amplitudes, left, right):
    return pl.pallas_call(
        compute_kernel,
        name="slot_updates",
        out_shape=(jax.ShapeDtypeStruct(BAND, F32), jax.ShapeDtypeStruct((2, N, N), F32)),
        in_specs=[SMEM] + [ANY] * 5,
        out_specs=(ANY, VMEM),
        scratch_shapes=[
            f32(2, 5, 2, N, 128), f32(2, N, N), f32(2, N, N), f32(2, N, N),
            pltpu.VMEM((1024, 1024), BF16), pltpu.VMEM((1024, 1024), BF16),
            pltpu.VMEM((1024, N), BF16), pltpu.VMEM((N, 1024), BF16),
            f32(N, N), f32(N, N), f32(TILES + 1, 2, N, 128), pltpu.SemaphoreType.DMA((7,)),
        ],
        compiler_params=params(),
    )(cols, band, probe, amplitudes, left, right)


def step_call(gather, grad, part, tile, probe, count):
    shapes = [jax.ShapeDtypeStruct(TILE, F32), jax.ShapeDtypeStruct((2, N, N), F32)]
    specs = [VMEM, ANY]
    if gather:
        shapes.append(jax.ShapeDtypeStruct(BAND, F32))
        specs.append(ANY)
    sends = REDUCE_SENDS + PROBE_SENDS + (GATHER_SENDS if gather else 0)
    return pl.pallas_call(
        functools.partial(step_kernel, gather),
        name="sum_and_gather" if gather else "sum_only",
        out_shape=tuple(shapes),
        in_specs=[ANY, ANY, VMEM, VMEM, VMEM],
        out_specs=tuple(specs),
        scratch_shapes=[
            f32(4, 4, *TILE), f32(4, 4, *TILE), f32(4, 2, 2, RB, 128), f32(4, 2, *TILE), f32(3, *TILE),
            f32(N, N), f32(N, N), f32(3, 128, N), f32(128, N), f32(3, 32, N), f32(32, N), f32(3, 8, N), f32(8, N),
            f32(5, 8, 128), f32(4, 3, 8, 128),
            pltpu.SemaphoreType.DMA((sends,)), pltpu.SemaphoreType.DMA((sends,)), pltpu.SemaphoreType.DMA((7,)),
        ],
        compiler_params=params(2 if gather else 3),
    )(grad.reshape(4, 2, 2, 2, N, 128), part, tile, probe, count)


def body(object_field, probe, scan_cols, amplitudes):
    left, right = (jnp.asarray(t) for t in tables())
    tile = object_field.reshape(2, RB, 2, 128).transpose(2, 0, 1, 3)
    count = jnp.full((8, 128), jnp.sum((scan_cols >= 0).astype(F32)))
    band = gather_call(tile)
    grad, part = compute_call(scan_cols, band, probe, amplitudes, left, right)
    tile, probe, band = step_call(True, grad, part, tile, probe, count)
    grad, part = compute_call(scan_cols, band, probe, amplitudes, left, right)
    tile, probe = step_call(False, grad, part, tile, probe, count)
    return tile.transpose(1, 2, 0, 3).reshape(2, RB, 256), probe


def solution(mesh):
    in_specs = (P(None, "obj", "pat"), P(), P(("obj", "pat")), P(("obj", "pat"), None, None))
    out_specs = (P(None, "obj", "pat"), P())
    return jax.shard_map(body, mesh=mesh, in_specs=in_specs, out_specs=out_specs, check_vma=False)
```

```python
import math

import jax
import jax.numpy as jnp
import ml_dtypes
import numpy as np
from jax import lax
from jax.experimental import pallas as pl
from jax.experimental.pallas import tpu as pltpu
from jax.sharding import PartitionSpec as P

N = 512
RB = 128
ITERS = 2
SLOTS = 2
GROUPS = 16
MESH = pl.DeviceIdType.MESH
F32 = jnp.float32
BF16 = jnp.bfloat16
TILE = (2, 2, RB, 128)
SENDS = 256


def tables():
    index = np.arange(N)
    angle = (index[:, None] * index[None, :] % N) * (2.0 * math.pi / N)
    real = np.cos(angle) / math.sqrt(N)
    imag = -np.sin(angle) / math.sqrt(N)
    left = np.block([[real, -imag], [imag, real]])
    right = np.block([[real, imag], [-imag, real]])
    return left.astype(ml_dtypes.bfloat16), right.astype(ml_dtypes.bfloat16)


def ring(value, step):
    return lax.rem(value + (step + 4), 4)


def rows_of(start, count):
    return pl.ds(pl.multiple_of(start, count), count)


class Links:
    def __init__(self, send_sems, recv_sems):
        self.send_sems, self.recv_sems, self.used, self.copies = send_sems, recv_sems, 0, []
        o, p = lax.axis_index("obj"), lax.axis_index("pat")
        self.o, self.p = o, p
        self.y, self.z, self.x, self.c = o // 4, lax.rem(o, 4), p // 2, lax.rem(p, 2)

    def target(self, dy=0, dz=0, dx=0, dc=0):
        core = self.c if dc == 0 else 1 - self.c
        return (ring(self.y, dy) * 4 + ring(self.z, dz), ring(self.x, dx) * 2 + core)

    def group(self, step):
        return (lax.rem(self.o + (step + GROUPS), GROUPS), self.p)

    def greet(self):
        near = [self.group(1), self.group(-1), self.target(dc=1)]
        for k in (1, 2, 3):
            near += [self.target(dy=k), self.target(dz=k), self.target(dx=k)]
        barrier = pltpu.get_barrier_semaphore()
        for device in near:
            pl.semaphore_signal(barrier, inc=1, device_id=device, device_id_type=MESH)
        pl.semaphore_wait(barrier, len(near))

    def send(self, src, dst, device):
        k = self.used
        self.used += 1
        copy = pltpu.make_async_remote_copy(
            src_ref=src, dst_ref=dst, send_sem=self.send_sems.at[k], recv_sem=self.recv_sems.at[k],
            device_id=device, device_id_type=MESH,
        )
        copy.start()
        self.copies.append(copy)
        return copy

    def drain(self):
        for copy in self.copies:
            copy.wait_send()
        self.copies = []


class Gather:
    def __init__(self, links, tile, bands):
        self.links, self.tile, self.bands = links, tile, bands
        x, c = links.x, links.c
        self.me = 2 * x + c
        self.sib, self.up, self.down = links.target(dc=1), links.target(dx=1), links.target(dx=-1)
        self.before, self.after, self.across = 2 * ring(x, -1) + c, 2 * ring(x, 1) + c, 2 * ring(x, 2) + c
        self.got = {}

    def at(self, b, pat, half=None):
        if half is None:
            return self.bands[b].at[pl.ds(2 * pat, 2)]
        return self.bands[b].at[pl.ds(2 * pat + half, 1)]

    def chain(self, b):
        src = self.tile if b == 0 else self.at(b, self.me)
        self.got["chain", b + 1] = self.links.send(src, self.at(b + 1, self.me), self.links.group(-1))

    def first(self, b):
        src = self.tile
        if b:
            self.got["chain", b].wait_recv()
            src = self.at(b, self.me)
        dst = self.at(b, self.me)
        self.got["up", b] = self.links.send(src, dst, self.up)
        self.got["down", b] = self.links.send(src, dst, self.down)
        if 0 < b < 3:
            self.chain(b)
        self.got["sib", b] = [self.links.send(src, dst, self.sib)]

    def second(self, b):
        for name, pat, half, onward in (("up", self.before, 0, self.up), ("down", self.after, 1, self.down)):
            self.got[name, b].wait_recv()
            part, whole = self.at(b, pat, half), self.at(b, pat)
            self.got[name + "2", b] = self.links.send(part, part, onward)
            self.got["sib", b].append(self.links.send(whole, whole, self.sib))

    def third(self, b):
        self.got["up2", b].wait_recv()
        self.got["down2", b].wait_recv()
        whole = self.at(b, self.across)
        self.got["sib", b].append(self.links.send(whole, whole, self.sib))

    def done(self, b):
        for copy in self.got["sib", b]:
            copy.wait_recv()


class Reduce:
    def __init__(self, links, own, theirs, sibs, halves, wholes, chained):
        self.links, self.own, self.theirs = links, own, theirs
        self.sibs, self.halves, self.wholes, self.chained = sibs, halves, wholes, chained
        self.sib, self.up, self.down = links.target(dc=1), links.target(dx=1), links.target(dx=-1)
        x = links.x
        self.before, self.after, self.across = ring(x, -1), ring(x, 1), ring(x, 2)
        self.got = {}

    def zeroth(self, b):
        self.got["sib", b] = self.links.send(self.theirs.at[b], self.sibs.at[b], self.sib)

    def first(self, b):
        own, sibs = self.own, self.sibs
        self.got["sib", b].wait_recv()

        @pl.loop(0, 4)
        def _(k):
            own[b, k] = own[b, k] + sibs[b, k]

        self.got["up", b] = self.links.send(own.at[b, self.across, 0], self.halves.at[b, 0], self.up)
        self.got["down", b] = self.links.send(own.at[b, self.across, 1], self.halves.at[b, 1], self.down)

    def second(self, b):
        own = self.own
        self.got["up", b].wait_recv()
        own[b, self.after, 0] = own[b, self.after, 0] + self.halves[b, 0]
        self.got["up2", b] = self.links.send(own.at[b, self.after], self.wholes.at[b, 0], self.up)
        self.got["down", b].wait_recv()
        own[b, self.before, 1] = own[b, self.before, 1] + self.halves[b, 1]
        self.got["down2", b] = self.links.send(own.at[b, self.before], self.wholes.at[b, 1], self.down)

    def third(self, b):
        own, x = self.own, self.links.x
        self.got["up2", b].wait_recv()
        self.got["down2", b].wait_recv()
        total = own[b, x] + (self.wholes[b, 0] + self.wholes[b, 1])
        if b < 3:
            self.got["chain", b].wait_recv()
            total = total + jnp.where(self.links.o > 0, self.chained[b], 0.0)
        if b:
            own[b, x] = total
            self.got["chain", b - 1] = self.links.send(own.at[b, x], self.chained.at[b - 1], self.links.group(1))
        return total


class ProbeSum:
    def __init__(self, links, grad, probe, bufs, counts, counted, need_count):
        self.links, self.grad, self.probe = links, grad, probe
        self.from_sib, self.r1, self.s1, self.r2, self.s2, self.r3 = bufs
        self.counts, self.counted, self.need = counts, counted, need_count
        self.sib = links.target(dc=1)
        self.got = []

    def pull(self):
        for copy in self.got:
            copy.wait_recv()
        self.got = []

    def put(self, src, dst, **step):
        self.got.append(self.links.send(src, dst, self.links.target(**step)))

    def count_out(self, n, axis):
        if self.need:
            for k in (1, 2, 3) if axis != "dc" else (1,):
                self.put(self.counts.at[n], self.counted.at[n, k - 1], **{axis: k})

    def count_in(self, n):
        if self.need:
            total = self.counts[n]
            for k in range(3 if n else 1):
                total = total + self.counted[n, k]
            self.counts[n + 1] = total

    def steps(self):
        links, grad, probe = self.links, self.grad, self.probe
        y, z, x, c = links.y, links.z, links.x, links.c
        lanes = (pl.ds(0, 256), pl.ds(256, 256))

        def start():
            self.put(grad.at[1 - c], self.from_sib, dc=1)
            self.count_out(0, "dc")

        def first():
            self.pull()
            self.count_in(0)

            @pl.loop(0, 8)
            def _(k):
                rows = rows_of(k * 64, 64)
                grad[c, rows, :] = grad[c, rows, :] + self.from_sib[rows, :]

            for k in (2, 1, 3):
                self.put(grad.at[c, rows_of(128 * ring(y, k), 128), lanes[0]], self.r1.at[0, k - 1], dy=k)
                self.put(grad.at[c, rows_of(128 * ring(z, k), 128), lanes[1]], self.r1.at[1, k - 1], dz=k)
            self.count_out(1, "dy")

        def second():
            self.pull()
            self.count_in(1)
            for h, place in ((0, y), (1, z)):
                total = grad[c, rows_of(128 * place, 128), lanes[h]]
                self.s1[h] = total + self.r1[h, 0] + self.r1[h, 1] + self.r1[h, 2]
            for k in (2, 1, 3):
                self.put(self.s1.at[0, rows_of(32 * ring(z, k), 32), :], self.r2.at[0, k - 1], dz=k)
                self.put(self.s1.at[1, rows_of(32 * ring(y, k), 32), :], self.r2.at[1, k - 1], dy=k)
            self.count_out(2, "dz")

        def third():
            self.pull()
            self.count_in(2)
            for h, place in ((0, z), (1, y)):
                total = self.s1[h, rows_of(32 * place, 32), :]
                self.s2[h] = total + self.r2[h, 0] + self.r2[h, 1] + self.r2[h, 2]
            for k in (2, 1, 3):
                self.put(self.s2.at[:, rows_of(8 * ring(x, k), 8), :], self.r3.at[k - 1], dx=k)
            self.count_out(3, "dx")

        def fourth():
            self.pull()
            self.count_in(3)
            total = self.s2[:, rows_of(8 * x, 8), :] + self.r3[0] + self.r3[1] + self.r3[2]
            count = self.counts[4][:, :1]
            for h, row in ((0, 128 * y + 32 * z + 8 * x), (1, 128 * z + 32 * y + 8 * x)):
                spot = rows_of(row, 8)
                probe[c, spot, lanes[h]] = probe[c, spot, lanes[h]] + total[h] / count
                for k in (2, 1, 3):
                    self.put(probe.at[c, spot, lanes[h]], probe.at[c, spot, lanes[h]], dx=k)

        def fifth():
            self.pull()
            for h, row, axis in ((0, 128 * y + 32 * z, "dz"), (1, 128 * z + 32 * y, "dy")):
                spot = probe.at[c, rows_of(row, 32), lanes[h]]
                for k in (2, 1, 3):
                    self.put(spot, spot, **{axis: k})

        def sixth():
            self.pull()
            for h, row, axis in ((0, 128 * y, "dy"), (1, 128 * z, "dz")):
                spot = probe.at[c, rows_of(row, 128), lanes[h]]
                for k in (2, 1, 3):
                    self.put(spot, spot, **{axis: k})

        def seventh():
            self.pull()
            self.put(probe.at[c], probe.at[c], dc=1)

        return [start, first, second, third, fourth, fifth, sixth, seventh, self.pull]


def kernel(cols, field, probe_in, amps, left, right, field_out, probe_out,
           band0, band1, band2, band3, tile, probe, amp, lt, rt, patch, flat, tall, wave, back, parts0, parts1,
           probe_grad, own, theirs, sibs, halves, wholes, chained,
           from_sib, r1, s1, r2, s2, r3, counts, counted, send_sems, recv_sems, sems):
    bands = (band0, band1, band2, band3)
    parts = (parts0, parts1)
    links = Links(send_sems, recv_sems)
    loads = [
        pltpu.make_async_copy(src, dst, sems.at[i])
        for i, (src, dst) in enumerate(((probe_in, probe), (left, lt), (right, rt), (amps, amp)))
    ]
    for load in loads:
        load.start()
    for t in range(2):
        tile[t] = field[:, :, 128 * t:128 * t + 128]
    for s in range(SLOTS):
        for edge in (0, 6):
            parts[s][edge] = jnp.zeros((2, RB, 128), F32)
    col = [jnp.maximum(cols[s], 0) for s in range(SLOTS)]
    base = [lax.div(col[s], 2) for s in range(SLOTS)]
    odd = [lax.rem(col[s], 2) == 1 for s in range(SLOTS)]
    valid = [(cols[s] >= 0).astype(F32) for s in range(SLOTS)]
    counts[0] = jnp.full((8, 128), valid[0] + valid[1], F32)
    lane = lax.broadcasted_iota(jnp.int32, (32, 128), 1)
    links.greet()

    def product(lhs, rhs):
        return jnp.dot(lhs, rhs, preferred_element_type=F32)

    def rows_in(b):
        inside = links.o + b < GROUPS
        for s in range(SLOTS):
            @pl.loop(0, 4)
            def _(m):
                rows = rows_of(m * 32, 32)
                whole = rows_of(b * RB + m * 32, 32)
                loaded = [[bands[b][jnp.minimum(base[s] + j, 15), part, rows, :] for j in range(5)] for part in (0, 1)]
                turned = [[pltpu.roll(v, 64, 1) for v in values] for values in loaded]
                for j in range(4):
                    cut = slice(128 * j, 128 * j + 128)
                    value = []
                    for part in range(2):
                        moved = jnp.where(lane < 64, turned[part][j], turned[part][j + 1])
                        v = jnp.where(inside, jnp.where(odd[s], moved, loaded[part][j]), 0.0)
                        patch[s, part, whole, cut] = v
                        value.append(v)
                    re, im = value
                    pre, pim = probe[0, whole, cut], probe[1, whole, cut]
                    flat[s, whole, cut] = (pre * re - pim * im).astype(BF16)
                    flat[s, whole, 512 + 128 * j:640 + 128 * j] = (pre * im + pim * re).astype(BF16)

            rows = slice(b * RB, b * RB + RB)
            mid = product(flat[s, rows, :], rt[...]).astype(BF16)
            tall[s, rows, :] = mid[:, :N]
            tall[s, N + b * RB:N + b * RB + RB, :] = mid[:, N:]

    def middle():
        for s in range(SLOTS):
            for n in range(2):
                cut = slice(256 * n, 256 * n + 256)
                wave[...] = product(lt[...], tall[s, :, cut])

                @pl.loop(0, 16)
                def _(m):
                    upper, lower = rows_of(m * 32, 32), rows_of(N + m * 32, 32)
                    re, im = wave[upper, :], wave[lower, :]
                    factor = amp[s, upper, cut] * lax.rsqrt(jnp.maximum(re * re + im * im, 0.0625))
                    tall[s, upper, cut] = (re * factor).astype(BF16)
                    tall[s, lower, cut] = (im * factor).astype(BF16)

                mid = product(rt[...], tall[s, :, cut]).astype(BF16)
                flat[s, :, cut] = mid[:N]
                flat[s, :, 512 + 256 * n:768 + 256 * n] = mid[N:]

    def rows_out(b):
        for s in range(SLOTS):
            back[...] = product(flat[s, b * RB:b * RB + RB, :], lt[...])

            @pl.loop(0, 4)
            def _(m):
                rows = rows_of(m * 32, 32)
                whole = rows_of(b * RB + m * 32, 32)
                last = [jnp.zeros((32, 128), F32)] * 2
                for j in range(5):
                    value = [jnp.zeros((32, 128), F32)] * 2
                    if j < 4:
                        cut = slice(128 * j, 128 * j + 128)
                        re, im = patch[s, 0, whole, cut], patch[s, 1, whole, cut]
                        pre, pim = probe[0, whole, cut], probe[1, whole, cut]
                        dre = (back[rows, cut] - (pre * re - pim * im)) * valid[s]
                        dim = (back[rows, 512 + 128 * j:640 + 128 * j] - (pre * im + pim * re)) * valid[s]
                        gre, gim = re * dre + im * dim, re * dim - im * dre
                        if s:
                            gre, gim = gre + probe_grad[0, whole, cut], gim + probe_grad[1, whole, cut]
                        probe_grad[0, whole, cut] = gre
                        probe_grad[1, whole, cut] = gim
                        value = [pre * dre + pim * dim, pre * dim - pim * dre]
                    for part in range(2):
                        turned = pltpu.roll(value[part], 64, 1) if j < 4 else value[part]
                        moved = jnp.where(lane < 64, last[part], turned)
                        last[part] = turned
                        parts[s][j + 1, part, rows, :] = jnp.where(odd[s], moved, value[part])

        def placed(t):
            spot = [jnp.clip(t - base[s], -1, 5) + 1 for s in range(SLOTS)]
            return parts[0][spot[0]] + parts[1][spot[1]]

        @pl.loop(0, 4)
        def _(k):
            for half in range(2):
                own[b, k, half] = placed(4 * k + 2 * links.c + half)
                theirs[b, k, half] = placed(4 * k + 2 * (1 - links.c) + half)

    for turn in range(ITERS):
        gather = Gather(links, tile, bands)
        gather.chain(0)
        gather.first(0)
        own_copy = pltpu.make_async_copy(tile, gather.at(0, gather.me), sems.at[4])
        own_copy.start()
        gather.second(0)
        gather.first(1)
        gather.third(0)
        if turn == 0:
            for load in loads:
                load.wait()
        else:
            tail[0]()
        own_copy.wait()
        gather.second(1)
        gather.first(2)
        if turn:
            tail[1]()
        gather.done(0)
        rows_in(0)
        gather.third(1)
        gather.second(2)
        gather.first(3)
        gather.done(1)
        rows_in(1)
        gather.third(2)
        gather.second(3)
        gather.done(2)
        rows_in(2)
        gather.third(3)
        gather.done(3)
        rows_in(3)
        links.drain()
        middle()
        reduce = Reduce(links, own, theirs, sibs, halves, wholes, chained)
        sums = ProbeSum(links, probe_grad, probe, (from_sib, r1, s1, r2, s2, r3), counts, counted, turn == 0).steps()
        rows_out(3)
        reduce.zeroth(3)
        rows_out(2)
        reduce.zeroth(2)
        reduce.first(3)
        rows_out(1)
        reduce.zeroth(1)
        reduce.first(2)
        reduce.second(3)
        rows_out(0)
        reduce.zeroth(0)
        sums[0]()
        reduce.first(1)
        sums[1]()
        reduce.second(2)
        reduce.third(3)
        reduce.first(0)
        sums[2]()
        reduce.second(1)
        sums[3]()
        reduce.third(2)
        sums[4]()
        reduce.second(0)
        sums[5]()
        reduce.third(1)
        sums[6]()
        total = reduce.third(0)
        tail = sums[7:]
        if turn < ITERS - 1:
            tile[...] = tile[...] + 0.25 * total
    for t in range(2):
        field_out[:, :, 128 * t:128 * t + 128] = tile[t] + 0.25 * total[t]
    tail[0]()
    mine = pltpu.make_async_copy(probe.at[links.c], probe_out.at[links.c], sems.at[5])
    mine.start()
    tail[1]()
    other = pltpu.make_async_copy(probe.at[1 - links.c], probe_out.at[1 - links.c], sems.at[6])
    other.start()
    links.drain()
    mine.wait()
    other.wait()


def f32(*shape):
    return pltpu.VMEM(shape, F32)


def body(object_field, probe, scan_cols, amplitudes):
    left, right = (jnp.asarray(t) for t in tables())
    anywhere = pl.BlockSpec(memory_space=pl.ANY)
    vmem = pl.BlockSpec(memory_space=pltpu.VMEM)
    return pl.pallas_call(
        kernel,
        name="reconstruct",
        out_shape=(jax.ShapeDtypeStruct((2, RB, 256), F32), jax.ShapeDtypeStruct((2, N, N), F32)),
        in_specs=[pl.BlockSpec(memory_space=pltpu.SMEM), vmem] + [anywhere] * 4,
        out_specs=(vmem, anywhere),
        scratch_shapes=[f32(16, 2, RB, 128)] * 4 + [
            f32(*TILE), f32(2, N, N), f32(2, N, N), pltpu.VMEM((1024, 1024), BF16), pltpu.VMEM((1024, 1024), BF16),
            f32(2, 2, N, N), pltpu.VMEM((2, N, 1024), BF16), pltpu.VMEM((2, 1024, N), BF16),
            f32(1024, 256), f32(RB, 1024), f32(7, 2, RB, 128), f32(7, 2, RB, 128),
            f32(2, N, N), f32(4, 4, *TILE), f32(4, 4, *TILE), f32(4, 4, *TILE),
            f32(4, 2, 2, RB, 128), f32(4, 2, *TILE), f32(3, *TILE),
            f32(N, N), f32(2, 3, 128, 256), f32(2, 128, 256), f32(2, 3, 32, 256), f32(2, 32, 256), f32(3, 2, 8, 256),
            f32(5, 8, 128), f32(4, 3, 8, 128),
            pltpu.SemaphoreType.DMA((SENDS,)), pltpu.SemaphoreType.DMA((SENDS,)), pltpu.SemaphoreType.DMA((7,)),
        ],
        compiler_params=pltpu.CompilerParams(vmem_limit_bytes=60 << 20, collective_id=1, has_side_effects=True),
    )(scan_cols, object_field, probe, amplitudes, left, right)


def solution(mesh):
    in_specs = (P(None, "obj", "pat"), P(), P(("obj", "pat")), P(("obj", "pat"), None, None))
    out_specs = (P(None, "obj", "pat"), P())
    return jax.shard_map(body, mesh=mesh, in_specs=in_specs, out_specs=out_specs, check_vma=False)
```

```python
import math

import jax
import jax.numpy as jnp
import ml_dtypes
import numpy as np
from jax import lax
from jax.experimental import pallas as pl
from jax.experimental.pallas import tpu as pltpu
from jax.sharding import PartitionSpec as P

N = 512
RB = 128
ITERS = 2
SLOTS = 2
GROUPS = 16
MESH = pl.DeviceIdType.MESH
F32 = jnp.float32
BF16 = jnp.bfloat16
TILE = (2, 2, RB, 128)
GATHER_SENDS, REDUCE_SENDS, PROBE_SENDS = 43, 34, 53


def tables():
    index = np.arange(N)
    angle = (index[:, None] * index[None, :] % N) * (2.0 * math.pi / N)
    real = np.cos(angle) / math.sqrt(N)
    imag = -np.sin(angle) / math.sqrt(N)
    left = np.block([[real, -imag], [imag, real]])
    right = np.block([[real, imag], [-imag, real]])
    return left.astype(ml_dtypes.bfloat16), right.astype(ml_dtypes.bfloat16)


def ring(value, step):
    return lax.rem(value + (step + 4), 4)


def rows_of(start, count):
    return pl.ds(pl.multiple_of(start, count), count)


class Links:
    def __init__(self, send_sems, recv_sems, base, limit):
        self.send_sems, self.recv_sems, self.copies = send_sems, recv_sems, []
        self.base, self.used, self.limit = base, base, base + limit
        o, p = lax.axis_index("obj"), lax.axis_index("pat")
        self.o, self.p = o, p
        self.y, self.z, self.x, self.c = o // 4, lax.rem(o, 4), p // 2, lax.rem(p, 2)

    def target(self, dy=0, dz=0, dx=0, dc=0):
        core = self.c if dc == 0 else 1 - self.c
        return (ring(self.y, dy) * 4 + ring(self.z, dz), ring(self.x, dx) * 2 + core)

    def group(self, step):
        return (lax.rem(self.o + (step + GROUPS), GROUPS), self.p)

    def greet(self):
        near = [self.group(1), self.group(-1), self.target(dc=1)]
        for k in (1, 2, 3):
            near += [self.target(dy=k), self.target(dz=k), self.target(dx=k)]
        barrier = pltpu.get_barrier_semaphore()
        for device in near:
            pl.semaphore_signal(barrier, inc=1, device_id=device, device_id_type=MESH)
        return lambda: pl.semaphore_wait(barrier, len(near))

    def send(self, src, dst, device):
        k = self.used
        self.used += 1
        assert k < self.limit
        copy = pltpu.make_async_remote_copy(
            src_ref=src, dst_ref=dst, send_sem=self.send_sems.at[k], recv_sem=self.recv_sems.at[k],
            device_id=device, device_id_type=MESH,
        )
        copy.start()
        self.copies.append(copy)
        return copy

    def drain(self):
        for copy in self.copies:
            copy.wait_send()
        self.copies, self.used = [], self.base


class Gather:
    def __init__(self, links, tile, bands):
        self.links, self.tile, self.bands = links, tile, bands
        x, c = links.x, links.c
        self.me = 2 * x + c
        self.sib, self.up, self.down = links.target(dc=1), links.target(dx=1), links.target(dx=-1)
        self.before, self.after, self.across = 2 * ring(x, -1) + c, 2 * ring(x, 1) + c, 2 * ring(x, 2) + c
        self.got = {}

    def at(self, b, pat, half=None):
        if half is None:
            return self.bands[b].at[pl.ds(2 * pat, 2)]
        return self.bands[b].at[pl.ds(2 * pat + half, 1)]

    def chain(self, b):
        src = self.tile if b == 0 else self.at(b, self.me)
        self.got["chain", b + 1] = self.links.send(src, self.at(b + 1, self.me), self.links.group(-1))

    def first(self, b):
        src = self.tile
        if b:
            self.got["chain", b].wait_recv()
            src = self.at(b, self.me)
        dst = self.at(b, self.me)
        for name, half, device in (("up", 0, self.up), ("down", 1, self.down), ("up'", 1, self.up), ("down'", 0, self.down)):
            part = pl.ds(half, 1)
            self.got[name, b] = self.links.send(src.at[part], dst.at[part], device)
        if 0 < b < 3:
            self.chain(b)
        self.got["sib", b] = [self.links.send(src, dst, self.sib)]

    def relay(self, b):
        for name, pat, half, onward in (("up", self.before, 0, self.up), ("down", self.after, 1, self.down)):
            self.got[name, b].wait_recv()
            part = self.at(b, pat, half)
            self.got[name + "2", b] = self.links.send(part, part, onward)

    def second(self, b):
        for name, pat in (("up'", self.before), ("down'", self.after)):
            self.got[name, b].wait_recv()
            whole = self.at(b, pat)
            self.got["sib", b].append(self.links.send(whole, whole, self.sib))

    def third(self, b):
        self.got["up2", b].wait_recv()
        self.got["down2", b].wait_recv()
        whole = self.at(b, self.across)
        self.got["sib", b].append(self.links.send(whole, whole, self.sib))

    def done(self, b):
        for copy in self.got["sib", b]:
            copy.wait_recv()


class Reduce:
    def __init__(self, links, own, theirs, sibs, halves, wholes, chained):
        self.links, self.own, self.theirs = links, own, theirs
        self.sibs, self.halves, self.wholes, self.chained = sibs, halves, wholes, chained
        self.sib, self.up, self.down = links.target(dc=1), links.target(dx=1), links.target(dx=-1)
        x = links.x
        self.before, self.after, self.across = ring(x, -1), ring(x, 1), ring(x, 2)
        self.pieces = (self.across, self.after, self.before, x)
        self.got = {}

    def zeroth(self, b):
        for piece, spot in enumerate(self.pieces if b == 3 else (None,)):
            at = (b,) if spot is None else (b, spot)
            self.got["sib", b, piece] = self.links.send(self.theirs.at[at], self.sibs.at[at], self.sib)

    def first(self, b):
        own, sibs = self.own, self.sibs

        def wait(piece):
            if b == 3:
                spot = self.pieces[piece]
                self.got["sib", b, piece].wait_recv()
                own[b, spot] = own[b, spot] + sibs[b, spot]

        def go(name, pat, half, dst, device):
            self.got[name, b] = self.links.send(own.at[b, pat, half], dst, device)

        if b < 3:
            self.got["sib", b, 0].wait_recv()

            @pl.loop(0, 4)
            def _(k):
                own[b, k] = own[b, k] + sibs[b, k]

        wait(0)
        go("up", self.across, 0, self.halves.at[b, 0], self.up)
        go("down", self.across, 1, self.halves.at[b, 1], self.down)
        wait(1)
        go("up'", self.after, 1, self.wholes.at[b, 0, 1], self.up)
        wait(2)
        go("down'", self.before, 0, self.wholes.at[b, 1, 0], self.down)
        wait(3)

    def second(self, b):
        own = self.own
        for name, pat, half, way, device in (("up", self.after, 0, 0, self.up), ("down", self.before, 1, 1, self.down)):
            self.got[name, b].wait_recv()
            own[b, pat, half] = own[b, pat, half] + self.halves[b, way]
            self.got[name + "2", b] = self.links.send(own.at[b, pat, half], self.wholes.at[b, way, half], device)

    def third(self, b):
        own, x = self.own, self.links.x
        for name in ("up'", "down'", "up2", "down2"):
            self.got[name, b].wait_recv()
        total = own[b, x] + (self.wholes[b, 0] + self.wholes[b, 1])
        if b < 3:
            self.got["chain", b].wait_recv()
            total = total + jnp.where(self.links.o > 0, self.chained[b], 0.0)
        if b:
            own[b, x] = total
            self.got["chain", b - 1] = self.links.send(own.at[b, x], self.chained.at[b - 1], self.links.group(1))
        return total


class ProbeSum:
    def __init__(self, links, grad, probe, bufs, counts, counted, need_count):
        self.axes = ("dy", "dz")
        self.links, self.grad, self.probe = links, grad, probe
        self.from_sib, self.r1, self.s1, self.r2, self.r3 = bufs
        self.counts, self.counted, self.need = counts, counted, need_count
        self.sib = links.target(dc=1)
        self.got = []

    def pull(self):
        for copy in self.got:
            copy.wait_recv()
        self.got = []

    def put(self, src, dst, **step):
        self.got.append(self.links.send(src, dst, self.links.target(**step)))

    def count_out(self, n, axis):
        if self.need:
            for k in (1, 2, 3) if axis != "dc" else (1,):
                self.put(self.counts.at[n], self.counted.at[n, k - 1], **{axis: k})

    def count_in(self, n):
        if self.need:
            total = self.counts[n]
            for k in range(3 if n else 1):
                total = total + self.counted[n, k]
            self.counts[n + 1] = total

    def steps(self):
        links, grad, probe = self.links, self.grad, self.probe
        y, z, x, c = links.y, links.z, links.x, links.c
        lanes = (pl.ds(0, 256), pl.ds(256, 256))
        outer = [(h, axis, y if axis == "dy" else z) for h, axis in enumerate(self.axes)]
        inner = [(h, "dz" if axis == "dy" else "dy", z if axis == "dy" else y) for h, axis in enumerate(self.axes)]
        block = [128 * place for _, _, place in outer]
        strip = [block[h] + 32 * place for h, _, place in inner]

        def piece(ref, plane, h, k):
            _, _, place = outer[h]
            return ref.at[plane + (rows_of(128 * ring(place, k), 128), lanes[h])]

        def start():
            for k in (2, 1, 3, 0):
                for h in range(2):
                    self.put(piece(grad, (1 - c,), h, k), piece(self.from_sib, (), h, k), dc=1)
            self.count_out(0, "dc")

        def first():
            arriving, self.got = self.got, []
            for n, (k, h) in enumerate((k, h) for k in (2, 1, 3, 0) for h in range(2)):
                arriving[n].wait_recv()
                _, axis, place = outer[h]
                rows = rows_of(128 * ring(place, k), 128)
                grad[c, rows, lanes[h]] = grad[c, rows, lanes[h]] + self.from_sib[rows, lanes[h]]
                if k:
                    self.put(piece(grad, (c,), h, k), self.r1.at[h, k - 1], **{axis: k})
            for copy in arriving[8:]:
                copy.wait_recv()
            self.count_in(0)
            self.count_out(1, "dy")

        def second():
            self.pull()
            self.count_in(1)
            for h in range(2):
                total = grad[c, rows_of(block[h], 128), lanes[h]]
                self.s1[h] = total + self.r1[h, 0] + self.r1[h, 1] + self.r1[h, 2]
            for k in (2, 1, 3):
                for h, axis, place in inner:
                    self.put(self.s1.at[h, rows_of(32 * ring(place, k), 32), :], self.r2.at[h, k - 1], **{axis: k})
            self.count_out(2, "dz")

        def third():
            self.pull()
            self.count_in(2)
            for h, _, place in inner:
                total = self.s1[h, rows_of(32 * place, 32), :]
                self.r3[x, h] = total + self.r2[h, 0] + self.r2[h, 1] + self.r2[h, 2]
            for k in (2, 1, 3):
                self.put(self.r3.at[x], self.r3.at[x], dx=k)
            self.count_out(3, "dx")

        def fourth():
            self.pull()
            self.count_in(3)
            count = self.counts[4][:1, :1]
            for h, axis, _ in inner:
                total = self.r3[0, h] + self.r3[1, h] + self.r3[2, h] + self.r3[3, h]
                rows = rows_of(strip[h], 32)
                probe[c, rows, lanes[h]] = probe[c, rows, lanes[h]] + total / count
                spot = probe.at[c, rows, lanes[h]]
                for k in (2, 1, 3):
                    self.put(spot, spot, **{axis: k})

        def fifth():
            self.pull()
            for k in (2, 1, 3):
                for h, axis, _ in outer:
                    self.put(piece(probe, (c,), h, 0), piece(probe, (c,), h, 0), **{axis: k})
            self.home = []
            self.onward(0)

        def sixth():
            arriving, self.got = self.got, []
            for n, k in enumerate((2, 1, 3)):
                for h in range(2):
                    arriving[2 * n + h].wait_recv()
                    self.onward(-k, (h,))

        def onward(k, parts=(0, 1)):
            for h in parts:
                spot = piece(probe, (c,), h, k)
                self.home.append(self.links.send(spot, spot, self.sib))

        def seventh():
            for copy in self.home:
                copy.wait_recv()

        self.onward = onward
        return [start, first, second, third, fourth, fifth, sixth, seventh]


def kernel(cols, field, probe_in, amps, left, right, field_out, probe_out,
           band0, band1, band2, band3, tile, probe, amp, lt, rt, patch, flat, tall, wave, back, parts0, parts1,
           probe_grad, own, theirs, sibs, halves, wholes, chained,
           from_sib, r1, s1, r2, r3, counts, counted, send_sems, recv_sems, sems):
    bands = (band0, band1, band2, band3)
    parts = (parts0, parts1)
    links = Links(send_sems, recv_sems, 0, GATHER_SENDS)
    sum_links = Links(send_sems, recv_sems, GATHER_SENDS, REDUCE_SENDS)
    probe_links = Links(send_sems, recv_sems, GATHER_SENDS + REDUCE_SENDS, PROBE_SENDS)
    met = links.greet()
    loads = [
        pltpu.make_async_copy(src, dst, sems.at[i])
        for i, (src, dst) in enumerate(((probe_in, probe), (left, lt), (right, rt), (amps, amp)))
    ]
    for load in loads:
        load.start()
    for t in range(2):
        tile[t] = field[:, :, 128 * t:128 * t + 128]
    for s in range(SLOTS):
        for edge in (0, 6):
            parts[s][edge] = jnp.zeros((2, RB, 128), F32)
    col = [jnp.maximum(cols[s], 0) for s in range(SLOTS)]
    base = [lax.div(col[s], 2) for s in range(SLOTS)]
    odd = [lax.rem(col[s], 2) == 1 for s in range(SLOTS)]
    valid = [(cols[s] >= 0).astype(F32) for s in range(SLOTS)]
    counts[0] = jnp.full((8, 128), valid[0] + valid[1], F32)
    lane = lax.broadcasted_iota(jnp.int32, (32, 128), 1)
    met()

    def product(lhs, rhs):
        return jnp.dot(lhs, rhs, preferred_element_type=F32)

    def rows_in(b):
        inside = links.o + b < GROUPS
        for s in range(SLOTS):
            @pl.loop(0, 4)
            def _(m):
                rows = rows_of(m * 32, 32)
                whole = rows_of(b * RB + m * 32, 32)
                loaded = [[bands[b][jnp.minimum(base[s] + j, 15), part, rows, :] for j in range(5)] for part in (0, 1)]
                turned = [[pltpu.roll(v, 64, 1) for v in values] for values in loaded]
                for j in range(4):
                    cut = slice(128 * j, 128 * j + 128)
                    value = []
                    for part in range(2):
                        moved = jnp.where(lane < 64, turned[part][j], turned[part][j + 1])
                        v = jnp.where(inside, jnp.where(odd[s], moved, loaded[part][j]), 0.0)
                        patch[s, part, whole, cut] = v
                        value.append(v)
                    re, im = value
                    pre, pim = probe[0, whole, cut], probe[1, whole, cut]
                    flat[s, whole, cut] = (pre * re - pim * im).astype(BF16)
                    flat[s, whole, 512 + 128 * j:640 + 128 * j] = (pre * im + pim * re).astype(BF16)

            rows = slice(b * RB, b * RB + RB)
            mid = product(flat[s, rows, :], rt[...]).astype(BF16)
            tall[s, rows, :] = mid[:, :N]
            tall[s, N + b * RB:N + b * RB + RB, :] = mid[:, N:]

    def middle():
        for s in range(SLOTS):
            for n in range(2):
                cut = slice(256 * n, 256 * n + 256)
                wave[...] = product(lt[...], tall[s, :, cut])

                @pl.loop(0, 16)
                def _(m):
                    upper, lower = rows_of(m * 32, 32), rows_of(N + m * 32, 32)
                    re, im = wave[upper, :], wave[lower, :]
                    factor = amp[s, upper, cut] * lax.rsqrt(jnp.maximum(re * re + im * im, 0.0625))
                    tall[s, upper, cut] = (re * factor).astype(BF16)
                    tall[s, lower, cut] = (im * factor).astype(BF16)

                mid = product(rt[...], tall[s, :, cut]).astype(BF16)
                flat[s, :, cut] = mid[:N]
                flat[s, :, 512 + 256 * n:768 + 256 * n] = mid[N:]

    def rows_out(b):
        for s in range(SLOTS):
            back[...] = product(flat[s, b * RB:b * RB + RB, :], lt[...])

            @pl.loop(0, 4)
            def _(m):
                rows = rows_of(m * 32, 32)
                whole = rows_of(b * RB + m * 32, 32)
                last = [jnp.zeros((32, 128), F32)] * 2
                for j in range(5):
                    value = [jnp.zeros((32, 128), F32)] * 2
                    if j < 4:
                        cut = slice(128 * j, 128 * j + 128)
                        re, im = patch[s, 0, whole, cut], patch[s, 1, whole, cut]
                        pre, pim = probe[0, whole, cut], probe[1, whole, cut]
                        dre = (back[rows, cut] - (pre * re - pim * im)) * valid[s]
                        dim = (back[rows, 512 + 128 * j:640 + 128 * j] - (pre * im + pim * re)) * valid[s]
                        gre, gim = re * dre + im * dim, re * dim - im * dre
                        if s:
                            gre, gim = gre + probe_grad[0, whole, cut], gim + probe_grad[1, whole, cut]
                        probe_grad[0, whole, cut] = gre
                        probe_grad[1, whole, cut] = gim
                        value = [pre * dre + pim * dim, pre * dim - pim * dre]
                    for part in range(2):
                        turned = pltpu.roll(value[part], 64, 1) if j < 4 else value[part]
                        moved = jnp.where(lane < 64, last[part], turned)
                        last[part] = turned
                        parts[s][j + 1, part, rows, :] = jnp.where(odd[s], moved, value[part])

        def placed(t):
            spot = [jnp.clip(t - base[s], -1, 5) + 1 for s in range(SLOTS)]
            return parts[0][spot[0]] + parts[1][spot[1]]

        @pl.loop(0, 4)
        def _(k):
            for half in range(2):
                own[b, k, half] = placed(4 * k + 2 * links.c + half)
                theirs[b, k, half] = placed(4 * k + 2 * (1 - links.c) + half)

    for turn in range(ITERS):
        gather = Gather(links, tile, bands)
        gather.chain(0)
        gather.first(0)
        own_copy = pltpu.make_async_copy(tile, gather.at(0, gather.me), sems.at[4])
        own_copy.start()
        gather.relay(0)
        gather.first(1)
        gather.second(0)
        if turn:
            p[6]()
        gather.third(0)
        gather.relay(1)
        if turn == 0:
            for load in loads:
                load.wait()
        gather.first(2)
        gather.second(1)
        own_copy.wait()
        gather.third(1)
        gather.relay(2)
        gather.first(3)
        if turn:
            p[7]()
        gather.done(0)
        rows_in(0)
        gather.second(2)
        gather.done(1)
        rows_in(1)
        gather.third(2)
        gather.relay(3)
        gather.done(2)
        rows_in(2)
        gather.second(3)
        gather.third(3)
        gather.done(3)
        rows_in(3)
        links.drain()
        middle()
        if turn:
            sum_links.drain()
            probe_links.drain()
        r = Reduce(sum_links, own, theirs, sibs, halves, wholes, chained)
        sums = ProbeSum(probe_links, probe_grad, probe, (from_sib, r1, s1, r2, r3), counts, counted, turn == 0)
        p = sums.steps()
        rows_out(3)
        r.zeroth(3)
        rows_out(2)
        r.zeroth(2)
        r.first(3)
        rows_out(1)
        r.zeroth(1)
        r.second(3)
        r.first(2)
        rows_out(0)
        p[0]()
        r.zeroth(0)
        if turn == 0:
            order = ((r.third, 3), p[1], (r.second, 2), (r.first, 1), (r.third, 2), (r.second, 1), p[2], (r.first, 0),
                     p[3], (r.third, 1), (r.second, 0), p[4], p[5], (r.third, 0))
        else:
            order = (p[1], (r.third, 3), (r.second, 2), (r.first, 1), p[2], (r.third, 2), p[3], (r.second, 1),
                     (r.first, 0), p[4], (r.third, 1), (r.second, 0), p[5], (r.third, 0), p[6])
        for step in order:
            if isinstance(step, tuple):
                total = step[0](step[1])
                if step == (r.third, 0):
                    tile[...] = tile[...] + 0.25 * total
            else:
                step()
    for t in range(2):
        field_out[:, :, 128 * t:128 * t + 128] = tile[t]
    mine = pltpu.make_async_copy(probe.at[links.c], probe_out.at[links.c], sems.at[5])
    mine.start()
    p[7]()
    other = pltpu.make_async_copy(probe.at[1 - links.c], probe_out.at[1 - links.c], sems.at[6])
    other.start()
    sum_links.drain()
    probe_links.drain()
    mine.wait()
    other.wait()


def hand_out(field, probe, field_out, probe_out, field_held, probe_held, sems):
    ways = [(field, field_held, field_out)]
    for k in range(8):
        part = (k // 4, pl.ds(128 * (k % 4), 128))
        ways.append((probe.at[part], probe_held.at[part], probe_out.at[part]))
    ins = [pltpu.make_async_copy(src, held, sems.at[0, k]) for k, (src, held, _) in enumerate(ways)]
    outs = [pltpu.make_async_copy(held, dst, sems.at[1, k]) for k, (_, held, dst) in enumerate(ways)]
    for copy in ins:
        copy.start()
    for arrived, onward in zip(ins, outs):
        arrived.wait()
        onward.start()
    for copy in outs:
        copy.wait()


def f32(*shape):
    return pltpu.VMEM(shape, F32)


def body(object_field, probe, scan_cols, amplitudes):
    left, right = (jnp.asarray(t) for t in tables())
    sends = GATHER_SENDS + REDUCE_SENDS + PROBE_SENDS
    anywhere = pl.BlockSpec(memory_space=pl.ANY)
    vmem = pl.BlockSpec(memory_space=pltpu.VMEM)
    field, probe = pl.pallas_call(
        kernel,
        name="reconstruct",
        out_shape=(jax.ShapeDtypeStruct((2, RB, 256), F32), jax.ShapeDtypeStruct((2, N, N), F32)),
        in_specs=[pl.BlockSpec(memory_space=pltpu.SMEM), vmem] + [anywhere] * 4,
        out_specs=(vmem, anywhere),
        scratch_shapes=[f32(16, 2, RB, 128)] * 4 + [
            f32(*TILE), f32(2, N, N), f32(2, N, N), pltpu.VMEM((1024, 1024), BF16), pltpu.VMEM((1024, 1024), BF16),
            f32(2, 2, N, N), pltpu.VMEM((2, N, 1024), BF16), pltpu.VMEM((2, 1024, N), BF16),
            f32(1024, 256), f32(RB, 1024), f32(7, 2, RB, 128), f32(7, 2, RB, 128),
            f32(2, N, N), f32(4, 4, *TILE), f32(4, 4, *TILE), f32(4, 4, *TILE),
            f32(4, 2, 2, RB, 128), f32(4, 2, *TILE), f32(3, *TILE),
            f32(N, N), f32(2, 3, 128, 256), f32(2, 128, 256), f32(2, 3, 32, 256), f32(4, 2, 32, 256),
            f32(5, 8, 128), f32(4, 3, 8, 128),
            pltpu.SemaphoreType.DMA((sends,)), pltpu.SemaphoreType.DMA((sends,)), pltpu.SemaphoreType.DMA((7,)),
        ],
        compiler_params=pltpu.CompilerParams(vmem_limit_bytes=60 << 20, collective_id=1, has_side_effects=True),
    )(scan_cols, object_field, probe, amplitudes, left, right)
    return pl.pallas_call(
        hand_out,
        name="hand_out",
        out_shape=(jax.ShapeDtypeStruct((2, RB, 256), F32), jax.ShapeDtypeStruct((2, N, N), F32)),
        in_specs=[anywhere] * 2,
        out_specs=(anywhere, anywhere),
        scratch_shapes=[f32(2, RB, 256), f32(2, N, N), pltpu.SemaphoreType.DMA((2, 9))],
        compiler_params=pltpu.CompilerParams(vmem_limit_bytes=16 << 20),
    )(field, probe)


def solution(mesh):
    in_specs = (P(None, "obj", "pat"), P(), P(("obj", "pat")), P(("obj", "pat"), None, None))
    out_specs = (P(None, "obj", "pat"), P())
    return jax.shard_map(body, mesh=mesh, in_specs=in_specs, out_specs=out_specs, check_vma=False)
```

```python
import math

import jax
import jax.numpy as jnp
import ml_dtypes
import numpy as np
from jax import lax
from jax.experimental import pallas as pl
from jax.experimental.pallas import tpu as pltpu
from jax.sharding import PartitionSpec as P

N = 512
RB = 128
ITERS = 2
SLOTS = 2
GROUPS = 16
MESH = pl.DeviceIdType.MESH
F32 = jnp.float32
BF16 = jnp.bfloat16
TILE = (2, 2, RB, 128)
GATHER_SENDS, REDUCE_SENDS, PROBE_SENDS = 43, 34, 53


def tables():
    index = np.arange(N)
    angle = (index[:, None] * index[None, :] % N) * (2.0 * math.pi / N)
    real = np.cos(angle) / math.sqrt(N)
    imag = -np.sin(angle) / math.sqrt(N)
    left = np.block([[real, -imag], [imag, real]])
    right = np.block([[real, imag], [-imag, real]])
    return left.astype(ml_dtypes.bfloat16), right.astype(ml_dtypes.bfloat16)


def ring(value, step):
    return lax.rem(value + (step + 4), 4)


def rows_of(start, count):
    if isinstance(start, int):
        return pl.ds(start, count)
    return pl.ds(pl.multiple_of(start, count), count)


class Links:
    def __init__(self, send_sems, recv_sems, base, limit):
        self.send_sems, self.recv_sems, self.copies = send_sems, recv_sems, []
        self.base, self.used, self.limit = base, base, base + limit
        o, p = lax.axis_index("obj"), lax.axis_index("pat")
        self.o, self.p = o, p
        self.y, self.z, self.x, self.c = o // 4, lax.rem(o, 4), p // 2, lax.rem(p, 2)

    def target(self, dy=0, dz=0, dx=0, dc=0):
        core = self.c if dc == 0 else 1 - self.c
        return (ring(self.y, dy) * 4 + ring(self.z, dz), ring(self.x, dx) * 2 + core)

    def group(self, step):
        return (lax.rem(self.o + (step + GROUPS), GROUPS), self.p)

    def greet(self):
        near = [self.group(1), self.group(-1), self.target(dc=1)]
        for k in (1, 2, 3):
            near += [self.target(dy=k), self.target(dz=k), self.target(dx=k)]
        barrier = pltpu.get_barrier_semaphore()
        for device in near:
            pl.semaphore_signal(barrier, inc=1, device_id=device, device_id_type=MESH)
        return lambda: pl.semaphore_wait(barrier, len(near))

    def send(self, src, dst, device):
        k = self.used
        self.used += 1
        assert k < self.limit
        copy = pltpu.make_async_remote_copy(
            src_ref=src, dst_ref=dst, send_sem=self.send_sems.at[k], recv_sem=self.recv_sems.at[k],
            device_id=device, device_id_type=MESH,
        )
        copy.start()
        self.copies.append(copy)
        return copy

    def drain(self):
        for copy in self.copies:
            copy.wait_send()
        self.copies, self.used = [], self.base


class Gather:
    def __init__(self, links, tile, bands):
        self.links, self.tile, self.bands = links, tile, bands
        x, c = links.x, links.c
        self.me = 2 * x + c
        self.sib, self.up, self.down = links.target(dc=1), links.target(dx=1), links.target(dx=-1)
        self.before, self.after, self.across = 2 * ring(x, -1) + c, 2 * ring(x, 1) + c, 2 * ring(x, 2) + c
        self.got = {}

    def at(self, b, pat, half=None):
        if half is None:
            return self.bands[b].at[pl.ds(2 * pat, 2)]
        return self.bands[b].at[pl.ds(2 * pat + half, 1)]

    def chain(self, b):
        src = self.tile if b == 0 else self.at(b, self.me)
        self.got["chain", b + 1] = self.links.send(src, self.at(b + 1, self.me), self.links.group(-1))

    def first(self, b):
        src = self.tile
        if b:
            self.got["chain", b].wait_recv()
            src = self.at(b, self.me)
        dst = self.at(b, self.me)
        for name, half, device in (("up", 0, self.up), ("down", 1, self.down), ("up'", 1, self.up), ("down'", 0, self.down)):
            part = pl.ds(half, 1)
            self.got[name, b] = self.links.send(src.at[part], dst.at[part], device)
        if 0 < b < 3:
            self.chain(b)
        self.got["sib", b] = [self.links.send(src, dst, self.sib)]

    def relay(self, b):
        for name, pat, half, onward in (("up", self.before, 0, self.up), ("down", self.after, 1, self.down)):
            self.got[name, b].wait_recv()
            part = self.at(b, pat, half)
            self.got[name + "2", b] = self.links.send(part, part, onward)

    def second(self, b):
        for name, pat in (("up'", self.before), ("down'", self.after)):
            self.got[name, b].wait_recv()
            whole = self.at(b, pat)
            self.got["sib", b].append(self.links.send(whole, whole, self.sib))

    def third(self, b):
        self.got["up2", b].wait_recv()
        self.got["down2", b].wait_recv()
        whole = self.at(b, self.across)
        self.got["sib", b].append(self.links.send(whole, whole, self.sib))

    def done(self, b):
        for copy in self.got["sib", b]:
            copy.wait_recv()


class Reduce:
    def __init__(self, links, own, theirs, sibs, halves, wholes, chained):
        self.links, self.own, self.theirs = links, own, theirs
        self.sibs, self.halves, self.wholes, self.chained = sibs, halves, wholes, chained
        self.sib, self.up, self.down = links.target(dc=1), links.target(dx=1), links.target(dx=-1)
        x = links.x
        self.before, self.after, self.across = ring(x, -1), ring(x, 1), ring(x, 2)
        self.pieces = (self.across, self.after, self.before, x)
        self.got = {}

    def zeroth(self, b):
        for piece, spot in enumerate(self.pieces if b == 3 else (None,)):
            at = (b,) if spot is None else (b, spot)
            self.got["sib", b, piece] = self.links.send(self.theirs.at[at], self.sibs.at[at], self.sib)

    def first(self, b):
        own, sibs = self.own, self.sibs

        def wait(piece):
            if b == 3:
                spot = self.pieces[piece]
                self.got["sib", b, piece].wait_recv()
                own[b, spot] = own[b, spot] + sibs[b, spot]

        def go(name, pat, half, dst, device):
            self.got[name, b] = self.links.send(own.at[b, pat, half], dst, device)

        if b < 3:
            self.got["sib", b, 0].wait_recv()

            @pl.loop(0, 4)
            def _(k):
                own[b, k] = own[b, k] + sibs[b, k]

        wait(0)
        go("up", self.across, 0, self.halves.at[b, 0], self.up)
        go("down", self.across, 1, self.halves.at[b, 1], self.down)
        wait(1)
        go("up'", self.after, 1, self.wholes.at[b, 0, 1], self.up)
        wait(2)
        go("down'", self.before, 0, self.wholes.at[b, 1, 0], self.down)
        wait(3)

    def second(self, b):
        own = self.own
        for name, pat, half, way, device in (("up", self.after, 0, 0, self.up), ("down", self.before, 1, 1, self.down)):
            self.got[name, b].wait_recv()
            own[b, pat, half] = own[b, pat, half] + self.halves[b, way]
            self.got[name + "2", b] = self.links.send(own.at[b, pat, half], self.wholes.at[b, way, half], device)

    def third(self, b):
        own, x = self.own, self.links.x
        for name in ("up'", "down'", "up2", "down2"):
            self.got[name, b].wait_recv()
        total = own[b, x] + (self.wholes[b, 0] + self.wholes[b, 1])
        if b < 3:
            self.got["chain", b].wait_recv()
            total = total + jnp.where(self.links.o > 0, self.chained[b], 0.0)
        if b:
            own[b, x] = total
            self.got["chain", b - 1] = self.links.send(own.at[b, x], self.chained.at[b - 1], self.links.group(1))
        return total


class ProbeSum:
    def __init__(self, links, grad, probe, bufs, counts, counted, need_count):
        self.axes = ("dy", "dz")
        self.links, self.grad, self.probe = links, grad, probe
        self.from_sib, self.r1, self.s1, self.r2, self.r3 = bufs
        self.counts, self.counted, self.need = counts, counted, need_count
        self.sib = links.target(dc=1)
        self.got = []

    def pull(self):
        for copy in self.got:
            copy.wait_recv()
        self.got = []

    def put(self, src, dst, **step):
        self.got.append(self.links.send(src, dst, self.links.target(**step)))

    def count_out(self, n, axis):
        if self.need:
            for k in (1, 2, 3) if axis != "dc" else (1,):
                self.put(self.counts.at[n], self.counted.at[n, k - 1], **{axis: k})

    def count_in(self, n):
        if self.need:
            total = self.counts[n]
            for k in range(3 if n else 1):
                total = total + self.counted[n, k]
            self.counts[n + 1] = total

    def steps(self):
        links, grad, probe = self.links, self.grad, self.probe
        y, z, x, c = links.y, links.z, links.x, links.c
        lanes = (pl.ds(0, 256), pl.ds(256, 256))
        outer = [(h, axis, y if axis == "dy" else z) for h, axis in enumerate(self.axes)]
        inner = [(h, "dz" if axis == "dy" else "dy", z if axis == "dy" else y) for h, axis in enumerate(self.axes)]
        block = [128 * place for _, _, place in outer]
        strip = [block[h] + 32 * place for h, _, place in inner]

        def piece(ref, plane, h, k):
            _, _, place = outer[h]
            return ref.at[plane + (rows_of(128 * ring(place, k), 128), lanes[h])]

        def start():
            for k in (2, 1, 3, 0):
                for h in range(2):
                    self.put(piece(grad, (1 - c,), h, k), piece(self.from_sib, (), h, k), dc=1)
            self.count_out(0, "dc")

        def first():
            arriving, self.got = self.got, []
            for n, (k, h) in enumerate((k, h) for k in (2, 1, 3, 0) for h in range(2)):
                arriving[n].wait_recv()
                _, axis, place = outer[h]
                rows = rows_of(128 * ring(place, k), 128)
                grad[c, rows, lanes[h]] = grad[c, rows, lanes[h]] + self.from_sib[rows, lanes[h]]
                if k:
                    self.put(piece(grad, (c,), h, k), self.r1.at[h, k - 1], **{axis: k})
            for copy in arriving[8:]:
                copy.wait_recv()
            self.count_in(0)
            self.count_out(1, "dy")

        def second():
            self.pull()
            self.count_in(1)
            for h in range(2):
                total = grad[c, rows_of(block[h], 128), lanes[h]]
                self.s1[h] = total + self.r1[h, 0] + self.r1[h, 1] + self.r1[h, 2]
            for k in (2, 1, 3):
                for h, axis, place in inner:
                    self.put(self.s1.at[h, rows_of(32 * ring(place, k), 32), :], self.r2.at[h, k - 1], **{axis: k})
            self.count_out(2, "dz")

        def third():
            self.pull()
            self.count_in(2)
            for h, _, place in inner:
                total = self.s1[h, rows_of(32 * place, 32), :]
                self.r3[x, h] = total + self.r2[h, 0] + self.r2[h, 1] + self.r2[h, 2]
            for k in (2, 1, 3):
                self.put(self.r3.at[x], self.r3.at[x], dx=k)
            self.count_out(3, "dx")

        def fourth():
            self.pull()
            self.count_in(3)
            count = self.counts[4][:1, :1]
            for h, axis, _ in inner:
                total = self.r3[0, h] + self.r3[1, h] + self.r3[2, h] + self.r3[3, h]
                rows = rows_of(strip[h], 32)
                probe[c, rows, lanes[h]] = probe[c, rows, lanes[h]] + total / count
                spot = probe.at[c, rows, lanes[h]]
                for k in (2, 1, 3):
                    self.put(spot, spot, **{axis: k})

        def fifth():
            self.pull()
            for k in (2, 1, 3):
                for h, axis, _ in outer:
                    self.put(piece(probe, (c,), h, 0), piece(probe, (c,), h, 0), **{axis: k})
            self.home = []
            self.onward(0)

        def sixth():
            arriving, self.got = self.got, []
            for n, k in enumerate((2, 1, 3)):
                for h in range(2):
                    arriving[2 * n + h].wait_recv()
                    self.onward(-k, (h,))

        def onward(k, parts=(0, 1)):
            for h in parts:
                spot = piece(probe, (c,), h, k)
                self.home.append(self.links.send(spot, spot, self.sib))

        def seventh():
            for copy in self.home:
                copy.wait_recv()

        self.onward = onward
        return [start, first, second, third, fourth, fifth, sixth, seventh]


def kernel(cols, field, probe_in, amps, left, right, field_out, probe_out,
           band0, band1, band2, band3, tile, probe, amp, lt, rt, patch, flat, tall, wave, back, parts0, parts1,
           probe_grad, own, theirs, sibs, halves, wholes, chained,
           from_sib, r1, s1, r2, r3, counts, counted, send_sems, recv_sems, sems):
    bands = (band0, band1, band2, band3)
    parts = (parts0, parts1)
    links = Links(send_sems, recv_sems, 0, GATHER_SENDS)
    sum_links = Links(send_sems, recv_sems, GATHER_SENDS, REDUCE_SENDS)
    probe_links = Links(send_sems, recv_sems, GATHER_SENDS + REDUCE_SENDS, PROBE_SENDS)
    met = links.greet()
    loads = [
        pltpu.make_async_copy(src, dst, sems.at[i])
        for i, (src, dst) in enumerate(((probe_in, probe), (left, lt), (right, rt), (amps, amp)))
    ]
    for load in loads:
        load.start()
    for t in range(2):
        tile[t] = field[:, :, 128 * t:128 * t + 128]
    for s in range(SLOTS):
        for edge in (0, 6):
            parts[s][edge] = jnp.zeros((2, RB, 128), F32)
    col = [jnp.maximum(cols[s], 0) for s in range(SLOTS)]
    base = [lax.div(col[s], 2) for s in range(SLOTS)]
    odd = [lax.rem(col[s], 2) == 1 for s in range(SLOTS)]
    valid = [(cols[s] >= 0).astype(F32) for s in range(SLOTS)]
    counts[0] = jnp.full((8, 128), valid[0] + valid[1], F32)
    lane = lax.broadcasted_iota(jnp.int32, (32, 128), 1)
    met()

    def product(lhs, rhs):
        return jnp.dot(lhs, rhs, preferred_element_type=F32)

    def rows_in(b):
        inside = links.o + b < GROUPS
        for s in range(SLOTS):
            for m in range(4):
                rows = rows_of(m * 32, 32)
                whole = rows_of(b * RB + m * 32, 32)
                loaded = [[bands[b][jnp.minimum(base[s] + j, 15), part, rows, :] for j in range(5)] for part in (0, 1)]
                turned = [[pltpu.roll(v, 64, 1) for v in values] for values in loaded]
                for j in range(4):
                    cut = slice(128 * j, 128 * j + 128)
                    value = []
                    for part in range(2):
                        moved = jnp.where(lane < 64, turned[part][j], turned[part][j + 1])
                        v = jnp.where(inside, jnp.where(odd[s], moved, loaded[part][j]), 0.0)
                        patch[s, part, whole, cut] = v
                        value.append(v)
                    re, im = value
                    pre, pim = probe[0, whole, cut], probe[1, whole, cut]
                    flat[s, whole, cut] = (pre * re - pim * im).astype(BF16)
                    flat[s, whole, 512 + 128 * j:640 + 128 * j] = (pre * im + pim * re).astype(BF16)

            rows = slice(b * RB, b * RB + RB)
            mid = product(flat[s, rows, :], rt[...]).astype(BF16)
            tall[s, rows, :] = mid[:, :N]
            tall[s, N + b * RB:N + b * RB + RB, :] = mid[:, N:]

    def middle():
        blocks = [(s, slice(256 * n, 256 * n + 256)) for s in range(SLOTS) for n in range(2)]

        def spread(i, r):
            s, cut = blocks[i]
            for start in (128 * r, N + 128 * r):
                wave[i % 2, start:start + 128, :] = product(lt[start:start + 128, :], tall[s, :, cut])

        def limit(i, r):
            s, cut = blocks[i]
            for m in range(128 * r, 128 * r + 128, 32):
                upper, lower = slice(m, m + 32), slice(N + m, N + m + 32)
                re, im = wave[i % 2, upper, :], wave[i % 2, lower, :]
                factor = amp[s, upper, cut] * lax.rsqrt(jnp.maximum(re * re + im * im, 0.0625))
                tall[s, upper, cut] = (re * factor).astype(BF16)
                tall[s, lower, cut] = (im * factor).astype(BF16)

        for r in range(4):
            spread(0, r)
        for i, (s, cut) in enumerate(blocks):
            for r in range(4):
                if i + 1 < len(blocks):
                    spread(i + 1, r)
                limit(i, r)
            for start in range(0, N, 256):
                rows = slice(start, start + 256)
                flat[s, rows, cut] = product(rt[rows, :], tall[s, :, cut]).astype(BF16)
                flat[s, rows, N + cut.start:N + cut.stop] = product(rt[N + start:N + start + 256, :], tall[s, :, cut]).astype(BF16)

    def rows_out(b):
        for s in range(SLOTS):
            back[...] = product(flat[s, b * RB:b * RB + RB, :], lt[...])

            for m in range(4):
                rows = rows_of(m * 32, 32)
                whole = rows_of(b * RB + m * 32, 32)
                last = [jnp.zeros((32, 128), F32)] * 2
                for j in range(5):
                    value = [jnp.zeros((32, 128), F32)] * 2
                    if j < 4:
                        cut = slice(128 * j, 128 * j + 128)
                        re, im = patch[s, 0, whole, cut], patch[s, 1, whole, cut]
                        pre, pim = probe[0, whole, cut], probe[1, whole, cut]
                        dre = (back[rows, cut] - (pre * re - pim * im)) * valid[s]
                        dim = (back[rows, 512 + 128 * j:640 + 128 * j] - (pre * im + pim * re)) * valid[s]
                        gre, gim = re * dre + im * dim, re * dim - im * dre
                        if s:
                            gre, gim = gre + probe_grad[0, whole, cut], gim + probe_grad[1, whole, cut]
                        probe_grad[0, whole, cut] = gre
                        probe_grad[1, whole, cut] = gim
                        value = [pre * dre + pim * dim, pre * dim - pim * dre]
                    for part in range(2):
                        turned = pltpu.roll(value[part], 64, 1) if j < 4 else value[part]
                        moved = jnp.where(lane < 64, last[part], turned)
                        last[part] = turned
                        parts[s][j + 1, part, rows, :] = jnp.where(odd[s], moved, value[part])

        def placed(t):
            spot = [jnp.clip(t - base[s], -1, 5) + 1 for s in range(SLOTS)]
            return parts[0][spot[0]] + parts[1][spot[1]]

        @pl.loop(0, 4)
        def _(k):
            for half in range(2):
                own[b, k, half] = placed(4 * k + 2 * links.c + half)
                theirs[b, k, half] = placed(4 * k + 2 * (1 - links.c) + half)

    for turn in range(ITERS):
        gather = Gather(links, tile, bands)
        gather.chain(0)
        gather.first(0)
        own_copy = pltpu.make_async_copy(tile, gather.at(0, gather.me), sems.at[4])
        own_copy.start()
        gather.relay(0)
        gather.first(1)
        gather.second(0)
        if turn:
            p[6]()
        gather.third(0)
        gather.relay(1)
        if turn == 0:
            for load in loads:
                load.wait()
        gather.first(2)
        gather.second(1)
        own_copy.wait()
        gather.third(1)
        gather.relay(2)
        gather.first(3)
        if turn:
            p[7]()
        gather.done(0)
        rows_in(0)
        gather.second(2)
        gather.done(1)
        rows_in(1)
        gather.third(2)
        gather.relay(3)
        gather.done(2)
        rows_in(2)
        gather.second(3)
        gather.third(3)
        gather.done(3)
        rows_in(3)
        links.drain()
        middle()
        if turn:
            sum_links.drain()
            probe_links.drain()
        r = Reduce(sum_links, own, theirs, sibs, halves, wholes, chained)
        sums = ProbeSum(probe_links, probe_grad, probe, (from_sib, r1, s1, r2, r3), counts, counted, turn == 0)
        p = sums.steps()
        rows_out(3)
        r.zeroth(3)
        rows_out(2)
        r.zeroth(2)
        r.first(3)
        rows_out(1)
        r.zeroth(1)
        r.second(3)
        r.first(2)
        rows_out(0)
        p[0]()
        r.zeroth(0)
        if turn == 0:
            order = ((r.third, 3), p[1], (r.second, 2), (r.first, 1), (r.third, 2), (r.second, 1), p[2], (r.first, 0),
                     p[3], (r.third, 1), (r.second, 0), p[4], p[5], (r.third, 0))
        else:
            order = (p[1], (r.third, 3), (r.second, 2), (r.first, 1), p[2], (r.third, 2), p[3], (r.second, 1),
                     (r.first, 0), p[4], (r.third, 1), (r.second, 0), p[5], (r.third, 0), p[6])
        for step in order:
            if isinstance(step, tuple):
                total = step[0](step[1])
                if step == (r.third, 0):
                    tile[...] = tile[...] + 0.25 * total
            else:
                step()
    for t in range(2):
        field_out[:, :, 128 * t:128 * t + 128] = tile[t]
    mine = pltpu.make_async_copy(probe.at[links.c], probe_out.at[links.c], sems.at[5])
    mine.start()
    p[7]()
    other = pltpu.make_async_copy(probe.at[1 - links.c], probe_out.at[1 - links.c], sems.at[6])
    other.start()
    sum_links.drain()
    probe_links.drain()
    mine.wait()
    other.wait()


def hand_out(field, probe, field_out, probe_out, field_held, probe_held, sems):
    ways = [(field, field_held, field_out)]
    for k in range(8):
        part = (k // 4, pl.ds(128 * (k % 4), 128))
        ways.append((probe.at[part], probe_held.at[part], probe_out.at[part]))
    ins = [pltpu.make_async_copy(src, held, sems.at[0, k]) for k, (src, held, _) in enumerate(ways)]
    outs = [pltpu.make_async_copy(held, dst, sems.at[1, k]) for k, (_, held, dst) in enumerate(ways)]
    for copy in ins:
        copy.start()
    for arrived, onward in zip(ins, outs):
        arrived.wait()
        onward.start()
    for copy in outs:
        copy.wait()


def f32(*shape):
    return pltpu.VMEM(shape, F32)


def body(object_field, probe, scan_cols, amplitudes):
    left, right = (jnp.asarray(t) for t in tables())
    sends = GATHER_SENDS + REDUCE_SENDS + PROBE_SENDS
    anywhere = pl.BlockSpec(memory_space=pl.ANY)
    vmem = pl.BlockSpec(memory_space=pltpu.VMEM)
    field, probe = pl.pallas_call(
        kernel,
        name="reconstruct",
        out_shape=(jax.ShapeDtypeStruct((2, RB, 256), F32), jax.ShapeDtypeStruct((2, N, N), F32)),
        in_specs=[pl.BlockSpec(memory_space=pltpu.SMEM), vmem] + [anywhere] * 4,
        out_specs=(vmem, anywhere),
        scratch_shapes=[f32(16, 2, RB, 128)] * 4 + [
            f32(*TILE), f32(2, N, N), f32(2, N, N), pltpu.VMEM((1024, 1024), BF16), pltpu.VMEM((1024, 1024), BF16),
            f32(2, 2, N, N), pltpu.VMEM((2, N, 1024), BF16), pltpu.VMEM((2, 1024, N), BF16),
            f32(2, 1024, 256), f32(RB, 1024), f32(7, 2, RB, 128), f32(7, 2, RB, 128),
            f32(2, N, N), f32(4, 4, *TILE), f32(4, 4, *TILE), f32(4, 4, *TILE),
            f32(4, 2, 2, RB, 128), f32(4, 2, *TILE), f32(3, *TILE),
            f32(N, N), f32(2, 3, 128, 256), f32(2, 128, 256), f32(2, 3, 32, 256), f32(4, 2, 32, 256),
            f32(5, 8, 128), f32(4, 3, 8, 128),
            pltpu.SemaphoreType.DMA((sends,)), pltpu.SemaphoreType.DMA((sends,)), pltpu.SemaphoreType.DMA((7,)),
        ],
        compiler_params=pltpu.CompilerParams(vmem_limit_bytes=60 << 20, collective_id=1, has_side_effects=True),
    )(scan_cols, object_field, probe, amplitudes, left, right)
    return pl.pallas_call(
        hand_out,
        name="hand_out",
        out_shape=(jax.ShapeDtypeStruct((2, RB, 256), F32), jax.ShapeDtypeStruct((2, N, N), F32)),
        in_specs=[anywhere] * 2,
        out_specs=(anywhere, anywhere),
        scratch_shapes=[f32(2, RB, 256), f32(2, N, N), pltpu.SemaphoreType.DMA((2, 9))],
        compiler_params=pltpu.CompilerParams(vmem_limit_bytes=16 << 20),
    )(field, probe)


def solution(mesh):
    in_specs = (P(None, "obj", "pat"), P(), P(("obj", "pat")), P(("obj", "pat"), None, None))
    out_specs = (P(None, "obj", "pat"), P())
    return jax.shard_map(body, mesh=mesh, in_specs=in_specs, out_specs=out_specs, check_vma=False)
```

```python
import math

import jax
import jax.numpy as jnp
import ml_dtypes
import numpy as np
from jax import lax
from jax.experimental import pallas as pl
from jax.experimental.pallas import tpu as pltpu
from jax.sharding import PartitionSpec as P

N = 512
RB = 128
ITERS = 2
SLOTS = 2
GROUPS = 16
MESH = pl.DeviceIdType.MESH
F32 = jnp.float32
BF16 = jnp.bfloat16
TILE = (2, 2, RB, 128)
GATHER_SENDS, REDUCE_SENDS, PROBE_SENDS = 43, 34, 53


def tables():
    index = np.arange(N)
    angle = (index[:, None] * index[None, :] % N) * (2.0 * math.pi / N)
    real = np.cos(angle) / math.sqrt(N)
    imag = -np.sin(angle) / math.sqrt(N)
    left = np.block([[real, -imag], [imag, real]])
    right = np.block([[real, imag], [-imag, real]])
    return left.astype(ml_dtypes.bfloat16), right.astype(ml_dtypes.bfloat16)


def ring(value, step):
    return lax.rem(value + (step + 4), 4)


def rows_of(start, count):
    if isinstance(start, int):
        return pl.ds(start, count)
    return pl.ds(pl.multiple_of(start, count), count)


class Links:
    def __init__(self, send_sems, recv_sems, base, limit):
        self.send_sems, self.recv_sems, self.copies = send_sems, recv_sems, []
        self.base, self.used, self.limit = base, base, base + limit
        o, p = lax.axis_index("obj"), lax.axis_index("pat")
        self.o, self.p = o, p
        self.y, self.z, self.x, self.c = o // 4, lax.rem(o, 4), p // 2, lax.rem(p, 2)

    def target(self, dy=0, dz=0, dx=0, dc=0):
        core = self.c if dc == 0 else 1 - self.c
        return (ring(self.y, dy) * 4 + ring(self.z, dz), ring(self.x, dx) * 2 + core)

    def group(self, step):
        return (lax.rem(self.o + (step + GROUPS), GROUPS), self.p)

    def greet(self):
        near = [self.group(1), self.group(-1), self.target(dc=1)]
        for k in (1, 2, 3):
            near += [self.target(dy=k), self.target(dz=k), self.target(dx=k)]
        barrier = pltpu.get_barrier_semaphore()
        for device in near:
            pl.semaphore_signal(barrier, inc=1, device_id=device, device_id_type=MESH)
        return lambda: pl.semaphore_wait(barrier, len(near))

    def send(self, src, dst, device):
        k = self.used
        self.used += 1
        assert k < self.limit
        copy = pltpu.make_async_remote_copy(
            src_ref=src, dst_ref=dst, send_sem=self.send_sems.at[k], recv_sem=self.recv_sems.at[k],
            device_id=device, device_id_type=MESH,
        )
        copy.start()
        self.copies.append(copy)
        return copy

    def drain(self):
        for copy in self.copies:
            copy.wait_send()
        self.copies, self.used = [], self.base


class Gather:
    def __init__(self, links, tile, bands):
        self.links, self.tile, self.bands = links, tile, bands
        x, c = links.x, links.c
        self.me = 2 * x + c
        self.sib, self.up, self.down = links.target(dc=1), links.target(dx=1), links.target(dx=-1)
        self.before, self.after, self.across = 2 * ring(x, -1) + c, 2 * ring(x, 1) + c, 2 * ring(x, 2) + c
        self.got = {}

    def at(self, b, pat, half=None):
        if half is None:
            return self.bands[b].at[pl.ds(2 * pat, 2)]
        return self.bands[b].at[pl.ds(2 * pat + half, 1)]

    def chain(self, b):
        src = self.tile if b == 0 else self.at(b, self.me)
        self.got["chain", b + 1] = self.links.send(src, self.at(b + 1, self.me), self.links.group(-1))

    def first(self, b):
        src = self.tile
        if b:
            self.got["chain", b].wait_recv()
            src = self.at(b, self.me)
        dst = self.at(b, self.me)
        for name, half, device in (("up", 0, self.up), ("down", 1, self.down), ("up'", 1, self.up), ("down'", 0, self.down)):
            part = pl.ds(half, 1)
            self.got[name, b] = self.links.send(src.at[part], dst.at[part], device)
        if 0 < b < 3:
            self.chain(b)
        self.got["sib", b] = [self.links.send(src, dst, self.sib)]

    def relay(self, b):
        for name, pat, half, onward in (("up", self.before, 0, self.up), ("down", self.after, 1, self.down)):
            self.got[name, b].wait_recv()
            part = self.at(b, pat, half)
            self.got[name + "2", b] = self.links.send(part, part, onward)

    def second(self, b):
        for name, pat in (("up'", self.before), ("down'", self.after)):
            self.got[name, b].wait_recv()
            whole = self.at(b, pat)
            self.got["sib", b].append(self.links.send(whole, whole, self.sib))

    def third(self, b):
        self.got["up2", b].wait_recv()
        self.got["down2", b].wait_recv()
        whole = self.at(b, self.across)
        self.got["sib", b].append(self.links.send(whole, whole, self.sib))

    def done(self, b):
        for copy in self.got["sib", b]:
            copy.wait_recv()


class Reduce:
    def __init__(self, links, own, theirs, sibs, halves, wholes, chained):
        self.links, self.own, self.theirs = links, own, theirs
        self.sibs, self.halves, self.wholes, self.chained = sibs, halves, wholes, chained
        self.sib, self.up, self.down = links.target(dc=1), links.target(dx=1), links.target(dx=-1)
        x = links.x
        self.before, self.after, self.across = ring(x, -1), ring(x, 1), ring(x, 2)
        self.pieces = (self.across, self.after, self.before, x)
        self.got = {}

    def zeroth(self, b):
        for piece, spot in enumerate(self.pieces if b == 3 else (None,)):
            at = (b,) if spot is None else (b, spot)
            self.got["sib", b, piece] = self.links.send(self.theirs.at[at], self.sibs.at[at], self.sib)

    def first(self, b):
        own, sibs = self.own, self.sibs

        def wait(piece):
            if b == 3:
                spot = self.pieces[piece]
                self.got["sib", b, piece].wait_recv()
                own[b, spot] = own[b, spot] + sibs[b, spot]

        def go(name, pat, half, dst, device):
            self.got[name, b] = self.links.send(own.at[b, pat, half], dst, device)

        if b < 3:
            self.got["sib", b, 0].wait_recv()

            @pl.loop(0, 4)
            def _(k):
                own[b, k] = own[b, k] + sibs[b, k]

        wait(0)
        go("up", self.across, 0, self.halves.at[b, 0], self.up)
        go("down", self.across, 1, self.halves.at[b, 1], self.down)
        wait(1)
        go("up'", self.after, 1, self.wholes.at[b, 0, 1], self.up)
        wait(2)
        go("down'", self.before, 0, self.wholes.at[b, 1, 0], self.down)
        wait(3)

    def second(self, b):
        own = self.own
        for name, pat, half, way, device in (("up", self.after, 0, 0, self.up), ("down", self.before, 1, 1, self.down)):
            self.got[name, b].wait_recv()
            own[b, pat, half] = own[b, pat, half] + self.halves[b, way]
            self.got[name + "2", b] = self.links.send(own.at[b, pat, half], self.wholes.at[b, way, half], device)

    def third(self, b):
        own, x = self.own, self.links.x
        for name in ("up'", "down'", "up2", "down2"):
            self.got[name, b].wait_recv()
        total = own[b, x] + (self.wholes[b, 0] + self.wholes[b, 1])
        if b < 3:
            self.got["chain", b].wait_recv()
            total = total + jnp.where(self.links.o > 0, self.chained[b], 0.0)
        if b:
            own[b, x] = total
            self.got["chain", b - 1] = self.links.send(own.at[b, x], self.chained.at[b - 1], self.links.group(1))
        return total


class ProbeSum:
    def __init__(self, links, grad, probe, bufs, counts, counted, need_count):
        self.axes = ("dy", "dz")
        self.links, self.grad, self.probe = links, grad, probe
        self.from_sib, self.r1, self.s1, self.r2, self.r3 = bufs
        self.counts, self.counted, self.need = counts, counted, need_count
        self.sib = links.target(dc=1)
        self.got = []

    def pull(self):
        for copy in self.got:
            copy.wait_recv()
        self.got = []

    def put(self, src, dst, **step):
        self.got.append(self.links.send(src, dst, self.links.target(**step)))

    def count_out(self, n, axis):
        if self.need:
            for k in (1, 2, 3) if axis != "dc" else (1,):
                self.put(self.counts.at[n], self.counted.at[n, k - 1], **{axis: k})

    def count_in(self, n):
        if self.need:
            total = self.counts[n]
            for k in range(3 if n else 1):
                total = total + self.counted[n, k]
            self.counts[n + 1] = total

    def steps(self):
        links, grad, probe = self.links, self.grad, self.probe
        y, z, x, c = links.y, links.z, links.x, links.c
        lanes = (pl.ds(0, 256), pl.ds(256, 256))
        outer = [(h, axis, y if axis == "dy" else z) for h, axis in enumerate(self.axes)]
        inner = [(h, "dz" if axis == "dy" else "dy", z if axis == "dy" else y) for h, axis in enumerate(self.axes)]
        block = [128 * place for _, _, place in outer]
        strip = [block[h] + 32 * place for h, _, place in inner]

        def piece(ref, plane, h, k):
            _, _, place = outer[h]
            return ref.at[plane + (rows_of(128 * ring(place, k), 128), lanes[h])]

        def start():
            for k in (2, 1, 3, 0):
                for h in range(2):
                    self.put(piece(grad, (1 - c,), h, k), piece(self.from_sib, (), h, k), dc=1)
            self.count_out(0, "dc")

        def first():
            arriving, self.got = self.got, []
            for n, (k, h) in enumerate((k, h) for k in (2, 1, 3, 0) for h in range(2)):
                arriving[n].wait_recv()
                _, axis, place = outer[h]
                rows = rows_of(128 * ring(place, k), 128)
                grad[c, rows, lanes[h]] = grad[c, rows, lanes[h]] + self.from_sib[rows, lanes[h]]
                if k:
                    self.put(piece(grad, (c,), h, k), self.r1.at[h, k - 1], **{axis: k})
            for copy in arriving[8:]:
                copy.wait_recv()
            self.count_in(0)
            self.count_out(1, "dy")

        def second():
            self.pull()
            self.count_in(1)
            for h in range(2):
                total = grad[c, rows_of(block[h], 128), lanes[h]]
                self.s1[h] = total + self.r1[h, 0] + self.r1[h, 1] + self.r1[h, 2]
            for k in (2, 1, 3):
                for h, axis, place in inner:
                    self.put(self.s1.at[h, rows_of(32 * ring(place, k), 32), :], self.r2.at[h, k - 1], **{axis: k})
            self.count_out(2, "dz")

        def third():
            self.pull()
            self.count_in(2)
            for h, _, place in inner:
                total = self.s1[h, rows_of(32 * place, 32), :]
                self.r3[x, h] = total + self.r2[h, 0] + self.r2[h, 1] + self.r2[h, 2]
            for k in (2, 1, 3):
                self.put(self.r3.at[x], self.r3.at[x], dx=k)
            self.count_out(3, "dx")

        def fourth():
            self.pull()
            self.count_in(3)
            count = self.counts[4][:1, :1]
            for h, axis, _ in inner:
                total = self.r3[0, h] + self.r3[1, h] + self.r3[2, h] + self.r3[3, h]
                rows = rows_of(strip[h], 32)
                probe[c, rows, lanes[h]] = probe[c, rows, lanes[h]] + total / count
                spot = probe.at[c, rows, lanes[h]]
                for k in (2, 1, 3):
                    self.put(spot, spot, **{axis: k})

        def fifth():
            self.pull()
            for k in (2, 1, 3):
                for h, axis, _ in outer:
                    self.put(piece(probe, (c,), h, 0), piece(probe, (c,), h, 0), **{axis: k})
            self.home = []
            self.onward(0)

        def sixth():
            arriving, self.got = self.got, []
            for n, k in enumerate((2, 1, 3)):
                for h in range(2):
                    arriving[2 * n + h].wait_recv()
                    self.onward(-k, (h,))

        def onward(k, parts=(0, 1)):
            for h in parts:
                spot = piece(probe, (c,), h, k)
                self.home.append(self.links.send(spot, spot, self.sib))

        def seventh():
            for copy in self.home:
                copy.wait_recv()

        self.onward = onward
        return [start, first, second, third, fourth, fifth, sixth, seventh]


def kernel(cols, field, probe_in, amps, left, right, field_out, probe_out,
           band0, band1, band2, band3, tile, probe, amp, lt, rt, patch, flat, tall, wave, back, parts0, parts1,
           probe_grad, own, theirs, sibs, halves, wholes, chained,
           from_sib, r1, s1, r2, r3, counts, counted, send_sems, recv_sems, sems):
    bands = (band0, band1, band2, band3)
    parts = (parts0, parts1)
    links = Links(send_sems, recv_sems, 0, GATHER_SENDS)
    sum_links = Links(send_sems, recv_sems, GATHER_SENDS, REDUCE_SENDS)
    probe_links = Links(send_sems, recv_sems, GATHER_SENDS + REDUCE_SENDS, PROBE_SENDS)
    met = links.greet()
    loads = [
        pltpu.make_async_copy(src, dst, sems.at[i])
        for i, (src, dst) in enumerate(((probe_in, probe), (left, lt), (right, rt), (amps, amp)))
    ]
    for load in loads:
        load.start()
    for t in range(2):
        tile[t] = field[:, :, 128 * t:128 * t + 128]
    for s in range(SLOTS):
        for edge in (0, 6):
            parts[s][edge] = jnp.zeros((2, RB, 128), F32)
    col = [jnp.maximum(cols[s], 0) for s in range(SLOTS)]
    base = [lax.div(col[s], 2) for s in range(SLOTS)]
    odd = [lax.rem(col[s], 2) == 1 for s in range(SLOTS)]
    valid = [(cols[s] >= 0).astype(F32) for s in range(SLOTS)]
    counts[0] = jnp.full((8, 128), valid[0] + valid[1], F32)
    lane = lax.broadcasted_iota(jnp.int32, (32, 128), 1)
    met()

    def product(lhs, rhs):
        return jnp.dot(lhs, rhs, preferred_element_type=F32)

    def rows_in(b):
        inside = links.o + b < GROUPS
        for s in range(SLOTS):
            for m in range(4):
                rows = rows_of(m * 32, 32)
                whole = rows_of(b * RB + m * 32, 32)
                loaded = [[bands[b][jnp.minimum(base[s] + j, 15), part, rows, :] for j in range(5)] for part in (0, 1)]
                turned = [[pltpu.roll(v, 64, 1) for v in values] for values in loaded]
                for j in range(4):
                    cut = slice(128 * j, 128 * j + 128)
                    value = []
                    for part in range(2):
                        moved = jnp.where(lane < 64, turned[part][j], turned[part][j + 1])
                        v = jnp.where(inside, jnp.where(odd[s], moved, loaded[part][j]), 0.0)
                        patch[s, part, whole, cut] = v
                        value.append(v)
                    re, im = value
                    pre, pim = probe[0, whole, cut], probe[1, whole, cut]
                    flat[s, whole, cut] = (pre * re - pim * im).astype(BF16)
                    flat[s, whole, 512 + 128 * j:640 + 128 * j] = (pre * im + pim * re).astype(BF16)

            rows = slice(b * RB, b * RB + RB)
            mid = product(flat[s, rows, :], rt[...]).astype(BF16)
            tall[s, rows, :] = mid[:, :N]
            tall[s, N + b * RB:N + b * RB + RB, :] = mid[:, N:]

    def middle():
        blocks = [(s, slice(256 * n, 256 * n + 256)) for s in range(SLOTS) for n in range(2)]

        def spread(i, r):
            s, cut = blocks[i]
            for start in (128 * r, N + 128 * r):
                wave[i % 2, start:start + 128, :] = product(lt[start:start + 128, :], tall[s, :, cut])

        def limit(i, r):
            s, cut = blocks[i]
            for m in range(128 * r, 128 * r + 128, 32):
                upper, lower = slice(m, m + 32), slice(N + m, N + m + 32)
                re, im = wave[i % 2, upper, :], wave[i % 2, lower, :]
                factor = amp[s, upper, cut] * lax.rsqrt(jnp.maximum(re * re + im * im, 0.0625))
                tall[s, upper, cut] = (re * factor).astype(BF16)
                tall[s, lower, cut] = (im * factor).astype(BF16)

        for r in range(4):
            spread(0, r)
        for i, (s, cut) in enumerate(blocks):
            for r in range(4):
                if i + 1 < len(blocks):
                    spread(i + 1, r)
                limit(i, r)
            for start in range(0, N, 256):
                rows = slice(start, start + 256)
                flat[s, rows, cut] = product(rt[rows, :], tall[s, :, cut]).astype(BF16)
                flat[s, rows, N + cut.start:N + cut.stop] = product(rt[N + start:N + start + 256, :], tall[s, :, cut]).astype(BF16)

    def rows_out(b):
        for s in range(SLOTS):
            back[...] = product(flat[s, b * RB:b * RB + RB, :], lt[...])

            for m in range(4):
                rows = rows_of(m * 32, 32)
                whole = rows_of(b * RB + m * 32, 32)
                last = [jnp.zeros((32, 128), F32)] * 2
                for j in range(5):
                    value = [jnp.zeros((32, 128), F32)] * 2
                    if j < 4:
                        cut = slice(128 * j, 128 * j + 128)
                        re, im = patch[s, 0, whole, cut], patch[s, 1, whole, cut]
                        pre, pim = probe[0, whole, cut], probe[1, whole, cut]
                        dre = (back[rows, cut] - (pre * re - pim * im)) * valid[s]
                        dim = (back[rows, 512 + 128 * j:640 + 128 * j] - (pre * im + pim * re)) * valid[s]
                        gre, gim = re * dre + im * dim, re * dim - im * dre
                        if s:
                            gre, gim = gre + probe_grad[0, whole, cut], gim + probe_grad[1, whole, cut]
                        probe_grad[0, whole, cut] = gre
                        probe_grad[1, whole, cut] = gim
                        value = [pre * dre + pim * dim, pre * dim - pim * dre]
                    for part in range(2):
                        turned = pltpu.roll(value[part], 64, 1) if j < 4 else value[part]
                        moved = jnp.where(lane < 64, last[part], turned)
                        last[part] = turned
                        parts[s][j + 1, part, rows, :] = jnp.where(odd[s], moved, value[part])

        def placed(t):
            spot = [jnp.clip(t - base[s], -1, 5) + 1 for s in range(SLOTS)]
            return parts[0][spot[0]] + parts[1][spot[1]]

        @pl.loop(0, 4)
        def _(k):
            for half in range(2):
                own[b, k, half] = placed(4 * k + 2 * links.c + half)
                theirs[b, k, half] = placed(4 * k + 2 * (1 - links.c) + half)

    for turn in range(ITERS):
        gather = Gather(links, tile, bands)
        gather.chain(0)
        gather.first(0)
        own_copy = pltpu.make_async_copy(tile, gather.at(0, gather.me), sems.at[4])
        own_copy.start()
        gather.relay(0)
        gather.first(1)
        if turn:
            p[5]()
        gather.second(0)
        gather.third(0)
        gather.relay(1)
        if turn == 0:
            for load in loads:
                load.wait()
        gather.first(2)
        gather.second(1)
        own_copy.wait()
        gather.third(1)
        gather.relay(2)
        gather.first(3)
        if turn:
            p[6]()
            p[7]()
        gather.done(0)
        rows_in(0)
        gather.second(2)
        gather.done(1)
        rows_in(1)
        gather.third(2)
        gather.relay(3)
        gather.done(2)
        rows_in(2)
        gather.second(3)
        gather.third(3)
        gather.done(3)
        rows_in(3)
        links.drain()
        middle()
        if turn:
            sum_links.drain()
            probe_links.drain()
        r = Reduce(sum_links, own, theirs, sibs, halves, wholes, chained)
        sums = ProbeSum(probe_links, probe_grad, probe, (from_sib, r1, s1, r2, r3), counts, counted, turn == 0)
        p = sums.steps()
        rows_out(3)
        r.zeroth(3)
        rows_out(2)
        r.zeroth(2)
        r.first(3)
        rows_out(1)
        rows_out(0)
        p[0]()
        r.zeroth(1)
        r.zeroth(0)
        r.second(3)
        r.first(2)
        if turn == 0:
            order = ((r.third, 3), p[1], (r.second, 2), (r.first, 1), (r.third, 2), (r.second, 1), p[2], (r.first, 0),
                     p[3], (r.third, 1), (r.second, 0), p[4], (r.third, 0))
        else:
            order = (p[1], (r.third, 3), (r.second, 2), (r.first, 1), p[2], (r.third, 2), p[3], (r.second, 1),
                     (r.first, 0), p[4], (r.third, 1), (r.second, 0), p[5], (r.third, 0), p[6])
        for step in order:
            if isinstance(step, tuple):
                total = step[0](step[1])
                if step == (r.third, 0):
                    tile[...] = tile[...] + 0.25 * total
            else:
                step()
    for t in range(2):
        field_out[:, :, 128 * t:128 * t + 128] = tile[t]
    mine = pltpu.make_async_copy(probe.at[links.c], probe_out.at[links.c], sems.at[5])
    mine.start()
    p[7]()
    other = pltpu.make_async_copy(probe.at[1 - links.c], probe_out.at[1 - links.c], sems.at[6])
    other.start()
    sum_links.drain()
    probe_links.drain()
    mine.wait()
    other.wait()


def hand_out(field, probe, field_out, probe_out, field_held, probe_held, sems):
    ways = [(field, field_held, field_out)]
    for k in range(8):
        part = (k // 4, pl.ds(128 * (k % 4), 128))
        ways.append((probe.at[part], probe_held.at[part], probe_out.at[part]))
    ins = [pltpu.make_async_copy(src, held, sems.at[0, k]) for k, (src, held, _) in enumerate(ways)]
    outs = [pltpu.make_async_copy(held, dst, sems.at[1, k]) for k, (_, held, dst) in enumerate(ways)]
    for copy in ins:
        copy.start()
    for arrived, onward in zip(ins, outs):
        arrived.wait()
        onward.start()
    for copy in outs:
        copy.wait()


def f32(*shape):
    return pltpu.VMEM(shape, F32)


def body(object_field, probe, scan_cols, amplitudes):
    left, right = (jnp.asarray(t) for t in tables())
    sends = GATHER_SENDS + REDUCE_SENDS + PROBE_SENDS
    anywhere = pl.BlockSpec(memory_space=pl.ANY)
    vmem = pl.BlockSpec(memory_space=pltpu.VMEM)
    field, probe = pl.pallas_call(
        kernel,
        name="reconstruct",
        out_shape=(jax.ShapeDtypeStruct((2, RB, 256), F32), jax.ShapeDtypeStruct((2, N, N), F32)),
        in_specs=[pl.BlockSpec(memory_space=pltpu.SMEM), vmem] + [anywhere] * 4,
        out_specs=(vmem, anywhere),
        scratch_shapes=[f32(16, 2, RB, 128)] * 4 + [
            f32(*TILE), f32(2, N, N), f32(2, N, N), pltpu.VMEM((1024, 1024), BF16), pltpu.VMEM((1024, 1024), BF16),
            f32(2, 2, N, N), pltpu.VMEM((2, N, 1024), BF16), pltpu.VMEM((2, 1024, N), BF16),
            f32(2, 1024, 256), f32(RB, 1024), f32(7, 2, RB, 128), f32(7, 2, RB, 128),
            f32(2, N, N), f32(4, 4, *TILE), f32(4, 4, *TILE), f32(4, 4, *TILE),
            f32(4, 2, 2, RB, 128), f32(4, 2, *TILE), f32(3, *TILE),
            f32(N, N), f32(2, 3, 128, 256), f32(2, 128, 256), f32(2, 3, 32, 256), f32(4, 2, 32, 256),
            f32(5, 8, 128), f32(4, 3, 8, 128),
            pltpu.SemaphoreType.DMA((sends,)), pltpu.SemaphoreType.DMA((sends,)), pltpu.SemaphoreType.DMA((7,)),
        ],
        compiler_params=pltpu.CompilerParams(vmem_limit_bytes=60 << 20, collective_id=1, has_side_effects=True),
    )(scan_cols, object_field, probe, amplitudes, left, right)
    return pl.pallas_call(
        hand_out,
        name="hand_out",
        out_shape=(jax.ShapeDtypeStruct((2, RB, 256), F32), jax.ShapeDtypeStruct((2, N, N), F32)),
        in_specs=[anywhere] * 2,
        out_specs=(anywhere, anywhere),
        scratch_shapes=[f32(2, RB, 256), f32(2, N, N), pltpu.SemaphoreType.DMA((2, 9))],
        compiler_params=pltpu.CompilerParams(vmem_limit_bytes=16 << 20),
    )(field, probe)


def solution(mesh):
    in_specs = (P(None, "obj", "pat"), P(), P(("obj", "pat")), P(("obj", "pat"), None, None))
    out_specs = (P(None, "obj", "pat"), P())
    return jax.shard_map(body, mesh=mesh, in_specs=in_specs, out_specs=out_specs, check_vma=False)
```

```python
import math

import jax
import jax.numpy as jnp
import ml_dtypes
import numpy as np
from jax import lax
from jax.experimental import pallas as pl
from jax.experimental.pallas import tpu as pltpu
from jax.sharding import PartitionSpec as P

N = 512
RB = 128
ITERS = 2
SLOTS = 2
GROUPS = 16
MESH = pl.DeviceIdType.MESH
F32 = jnp.float32
BF16 = jnp.bfloat16
TILE = (2, 2, RB, 128)
GATHER_SENDS, REDUCE_SENDS, PROBE_SENDS = 43, 34, 53


def tables():
    index = np.arange(N)
    angle = (index[:, None] * index[None, :] % N) * (2.0 * math.pi / N)
    real = np.cos(angle) / math.sqrt(N)
    imag = -np.sin(angle) / math.sqrt(N)
    left = np.block([[real, -imag], [imag, real]])
    right = np.block([[real, imag], [-imag, real]])
    return left.astype(ml_dtypes.bfloat16), right.astype(ml_dtypes.bfloat16)


def ring(value, step):
    return lax.rem(value + (step + 4), 4)


def rows_of(start, count):
    if isinstance(start, int):
        return pl.ds(start, count)
    return pl.ds(pl.multiple_of(start, count), count)


class Links:
    def __init__(self, send_sems, recv_sems, base, limit):
        self.send_sems, self.recv_sems, self.copies = send_sems, recv_sems, []
        self.base, self.used, self.limit = base, base, base + limit
        o, p = lax.axis_index("obj"), lax.axis_index("pat")
        self.o, self.p = o, p
        self.y, self.z, self.x, self.c = o // 4, lax.rem(o, 4), p // 2, lax.rem(p, 2)

    def target(self, dy=0, dz=0, dx=0, dc=0):
        core = self.c if dc == 0 else 1 - self.c
        return (ring(self.y, dy) * 4 + ring(self.z, dz), ring(self.x, dx) * 2 + core)

    def group(self, step):
        return (lax.rem(self.o + (step + GROUPS), GROUPS), self.p)

    def greet(self):
        near = [self.group(1), self.group(-1), self.target(dc=1)]
        for k in (1, 2, 3):
            near += [self.target(dy=k), self.target(dz=k), self.target(dx=k)]
        barrier = pltpu.get_barrier_semaphore()
        for device in near:
            pl.semaphore_signal(barrier, inc=1, device_id=device, device_id_type=MESH)
        return lambda: pl.semaphore_wait(barrier, len(near))

    def send(self, src, dst, device):
        k = self.used
        self.used += 1
        assert k < self.limit
        copy = pltpu.make_async_remote_copy(
            src_ref=src, dst_ref=dst, send_sem=self.send_sems.at[k], recv_sem=self.recv_sems.at[k],
            device_id=device, device_id_type=MESH,
        )
        copy.start()
        self.copies.append(copy)
        return copy

    def drain(self):
        for copy in self.copies:
            copy.wait_send()
        self.copies, self.used = [], self.base


class Gather:
    def __init__(self, links, tile, bands):
        self.links, self.tile, self.bands = links, tile, bands
        x, c = links.x, links.c
        self.me = 2 * x + c
        self.sib, self.up, self.down = links.target(dc=1), links.target(dx=1), links.target(dx=-1)
        self.before, self.after, self.across = 2 * ring(x, -1) + c, 2 * ring(x, 1) + c, 2 * ring(x, 2) + c
        self.got = {}

    def at(self, b, pat, half=None):
        if half is None:
            return self.bands[b].at[pl.ds(2 * pat, 2)]
        return self.bands[b].at[pl.ds(2 * pat + half, 1)]

    def chain(self, b):
        src = self.tile if b == 0 else self.at(b, self.me)
        self.got["chain", b + 1] = self.links.send(src, self.at(b + 1, self.me), self.links.group(-1))

    def first(self, b):
        src = self.tile
        if b:
            self.got["chain", b].wait_recv()
            src = self.at(b, self.me)
        dst = self.at(b, self.me)
        for name, half, device in (("up", 0, self.up), ("down", 1, self.down), ("up'", 1, self.up), ("down'", 0, self.down)):
            part = pl.ds(half, 1)
            self.got[name, b] = self.links.send(src.at[part], dst.at[part], device)
        if 0 < b < 3:
            self.chain(b)
        self.got["sib", b] = [self.links.send(src, dst, self.sib)]

    def relay(self, b):
        for name, pat, half, onward in (("up", self.before, 0, self.up), ("down", self.after, 1, self.down)):
            self.got[name, b].wait_recv()
            part = self.at(b, pat, half)
            self.got[name + "2", b] = self.links.send(part, part, onward)

    def second(self, b):
        for name, pat in (("up'", self.before), ("down'", self.after)):
            self.got[name, b].wait_recv()
            whole = self.at(b, pat)
            self.got["sib", b].append(self.links.send(whole, whole, self.sib))

    def third(self, b):
        self.got["up2", b].wait_recv()
        self.got["down2", b].wait_recv()
        whole = self.at(b, self.across)
        self.got["sib", b].append(self.links.send(whole, whole, self.sib))

    def done(self, b):
        for copy in self.got["sib", b]:
            copy.wait_recv()


class Reduce:
    def __init__(self, links, own, theirs, sibs, halves, wholes, chained):
        self.links, self.own, self.theirs = links, own, theirs
        self.sibs, self.halves, self.wholes, self.chained = sibs, halves, wholes, chained
        self.sib, self.up, self.down = links.target(dc=1), links.target(dx=1), links.target(dx=-1)
        x = links.x
        self.before, self.after, self.across = ring(x, -1), ring(x, 1), ring(x, 2)
        self.pieces = (self.across, self.after, self.before, x)
        self.got = {}

    def zeroth(self, b):
        for piece, spot in enumerate(self.pieces if b == 3 else (None,)):
            at = (b,) if spot is None else (b, spot)
            self.got["sib", b, piece] = self.links.send(self.theirs.at[at], self.sibs.at[at], self.sib)

    def first(self, b):
        own, sibs = self.own, self.sibs

        def wait(piece):
            if b == 3:
                spot = self.pieces[piece]
                self.got["sib", b, piece].wait_recv()
                own[b, spot] = own[b, spot] + sibs[b, spot]

        def go(name, pat, half, dst, device):
            self.got[name, b] = self.links.send(own.at[b, pat, half], dst, device)

        if b < 3:
            self.got["sib", b, 0].wait_recv()

            @pl.loop(0, 4)
            def _(k):
                own[b, k] = own[b, k] + sibs[b, k]

        wait(0)
        go("up", self.across, 0, self.halves.at[b, 0], self.up)
        go("down", self.across, 1, self.halves.at[b, 1], self.down)
        wait(1)
        go("up'", self.after, 1, self.wholes.at[b, 0, 1], self.up)
        wait(2)
        go("down'", self.before, 0, self.wholes.at[b, 1, 0], self.down)
        wait(3)

    def second(self, b):
        own = self.own
        for name, pat, half, way, device in (("up", self.after, 0, 0, self.up), ("down", self.before, 1, 1, self.down)):
            self.got[name, b].wait_recv()
            own[b, pat, half] = own[b, pat, half] + self.halves[b, way]
            self.got[name + "2", b] = self.links.send(own.at[b, pat, half], self.wholes.at[b, way, half], device)

    def third(self, b):
        own, x = self.own, self.links.x
        for name in ("up'", "down'", "up2", "down2"):
            self.got[name, b].wait_recv()
        total = own[b, x] + (self.wholes[b, 0] + self.wholes[b, 1])
        if b < 3:
            self.got["chain", b].wait_recv()
            total = total + jnp.where(self.links.o > 0, self.chained[b], 0.0)
        if b:
            own[b, x] = total
            self.got["chain", b - 1] = self.links.send(own.at[b, x], self.chained.at[b - 1], self.links.group(1))
        return total


class ProbeSum:
    def __init__(self, links, grad, probe, bufs, counts, counted, need_count):
        self.axes = ("dy", "dz")
        self.links, self.grad, self.probe = links, grad, probe
        self.from_sib, self.r1, self.s1, self.r2, self.r3 = bufs
        self.counts, self.counted, self.need = counts, counted, need_count
        self.sib = links.target(dc=1)
        self.got = []

    def pull(self):
        for copy in self.got:
            copy.wait_recv()
        self.got = []

    def put(self, src, dst, **step):
        self.got.append(self.links.send(src, dst, self.links.target(**step)))

    def count_out(self, n, axis):
        if self.need:
            for k in (1, 2, 3) if axis != "dc" else (1,):
                self.put(self.counts.at[n], self.counted.at[n, k - 1], **{axis: k})

    def count_in(self, n):
        if self.need:
            total = self.counts[n]
            for k in range(3 if n else 1):
                total = total + self.counted[n, k]
            self.counts[n + 1] = total

    def steps(self):
        links, grad, probe = self.links, self.grad, self.probe
        y, z, x, c = links.y, links.z, links.x, links.c
        lanes = (pl.ds(0, 256), pl.ds(256, 256))
        outer = [(h, axis, y if axis == "dy" else z) for h, axis in enumerate(self.axes)]
        inner = [(h, "dz" if axis == "dy" else "dy", z if axis == "dy" else y) for h, axis in enumerate(self.axes)]
        block = [128 * place for _, _, place in outer]
        strip = [block[h] + 32 * place for h, _, place in inner]

        def piece(ref, plane, h, k):
            _, _, place = outer[h]
            return ref.at[plane + (rows_of(128 * ring(place, k), 128), lanes[h])]

        def start():
            for k in (2, 1, 3, 0):
                for h in range(2):
                    self.put(piece(grad, (1 - c,), h, k), piece(self.from_sib, (), h, k), dc=1)
            self.count_out(0, "dc")

        def first():
            arriving, self.got = self.got, []
            for n, (k, h) in enumerate((k, h) for k in (2, 1, 3, 0) for h in range(2)):
                arriving[n].wait_recv()
                _, axis, place = outer[h]
                rows = rows_of(128 * ring(place, k), 128)
                grad[c, rows, lanes[h]] = grad[c, rows, lanes[h]] + self.from_sib[rows, lanes[h]]
                if k:
                    self.put(piece(grad, (c,), h, k), self.r1.at[h, k - 1], **{axis: k})
            for copy in arriving[8:]:
                copy.wait_recv()
            self.count_in(0)
            self.count_out(1, "dy")

        def second():
            self.pull()
            self.count_in(1)
            for h in range(2):
                total = grad[c, rows_of(block[h], 128), lanes[h]]
                self.s1[h] = total + self.r1[h, 0] + self.r1[h, 1] + self.r1[h, 2]
            for k in (2, 1, 3):
                for h, axis, place in inner:
                    self.put(self.s1.at[h, rows_of(32 * ring(place, k), 32), :], self.r2.at[h, k - 1], **{axis: k})
            self.count_out(2, "dz")

        def third():
            self.pull()
            self.count_in(2)
            for h, _, place in inner:
                total = self.s1[h, rows_of(32 * place, 32), :]
                self.r3[x, h] = total + self.r2[h, 0] + self.r2[h, 1] + self.r2[h, 2]
            for k in (2, 1, 3):
                self.put(self.r3.at[x], self.r3.at[x], dx=k)
            self.count_out(3, "dx")

        def fourth():
            self.pull()
            self.count_in(3)
            count = self.counts[4][:1, :1]
            for h, axis, _ in inner:
                total = self.r3[0, h] + self.r3[1, h] + self.r3[2, h] + self.r3[3, h]
                rows = rows_of(strip[h], 32)
                probe[c, rows, lanes[h]] = probe[c, rows, lanes[h]] + total / count
                spot = probe.at[c, rows, lanes[h]]
                for k in (2, 1, 3):
                    self.put(spot, spot, **{axis: k})

        def fifth():
            self.pull()
            for k in (2, 1, 3):
                for h, axis, _ in outer:
                    self.put(piece(probe, (c,), h, 0), piece(probe, (c,), h, 0), **{axis: k})
            self.home = []
            self.onward(0)

        def sixth():
            arriving, self.got = self.got, []
            for n, k in enumerate((2, 1, 3)):
                for h in range(2):
                    arriving[2 * n + h].wait_recv()
                    self.onward(-k, (h,))

        def onward(k, parts=(0, 1)):
            for h in parts:
                spot = piece(probe, (c,), h, k)
                self.home.append(self.links.send(spot, spot, self.sib))

        def seventh():
            for copy in self.home:
                copy.wait_recv()

        self.onward = onward
        return [start, first, second, third, fourth, fifth, sixth, seventh]


def kernel(cols, field, probe_in, amps, left, right, field_out, probe_out,
           band0, band1, band2, band3, tile, probe, amp, lt, rt, patch, flat, tall, wave, back, parts0, parts1,
           probe_grad, own, theirs, sibs, halves, wholes, chained,
           from_sib, r1, s1, r2, r3, counts, counted, send_sems, recv_sems, sems):
    bands = (band0, band1, band2, band3)
    parts = (parts0, parts1)
    links = Links(send_sems, recv_sems, 0, GATHER_SENDS)
    sum_links = Links(send_sems, recv_sems, GATHER_SENDS, REDUCE_SENDS)
    probe_links = Links(send_sems, recv_sems, GATHER_SENDS + REDUCE_SENDS, PROBE_SENDS)
    met = links.greet()
    loads = [
        pltpu.make_async_copy(src, dst, sems.at[i])
        for i, (src, dst) in enumerate(((probe_in, probe), (left, lt), (right, rt), (amps, amp)))
    ]
    for load in loads:
        load.start()
    for t in range(2):
        tile[t] = field[:, :, 128 * t:128 * t + 128]
    for s in range(SLOTS):
        for edge in (0, 6):
            parts[s][edge] = jnp.zeros((2, RB, 128), F32)
    col = [jnp.maximum(cols[s], 0) for s in range(SLOTS)]
    base = [lax.div(col[s], 2) for s in range(SLOTS)]
    odd = [lax.rem(col[s], 2) == 1 for s in range(SLOTS)]
    valid = [(cols[s] >= 0).astype(F32) for s in range(SLOTS)]
    counts[0] = jnp.full((8, 128), valid[0] + valid[1], F32)
    lane = lax.broadcasted_iota(jnp.int32, (32, 128), 1)
    met()

    def product(lhs, rhs):
        return jnp.dot(lhs, rhs, preferred_element_type=F32)

    def rows_in(b):
        inside = links.o + b < GROUPS
        for s in range(SLOTS):
            for m in range(4):
                rows = rows_of(m * 32, 32)
                whole = rows_of(b * RB + m * 32, 32)
                loaded = [[bands[b][jnp.minimum(base[s] + j, 15), part, rows, :] for j in range(5)] for part in (0, 1)]
                turned = [[pltpu.roll(v, 64, 1) for v in values] for values in loaded]
                for j in range(4):
                    cut = slice(128 * j, 128 * j + 128)
                    value = []
                    for part in range(2):
                        moved = jnp.where(lane < 64, turned[part][j], turned[part][j + 1])
                        v = jnp.where(inside, jnp.where(odd[s], moved, loaded[part][j]), 0.0)
                        patch[s, part, whole, cut] = v
                        value.append(v)
                    re, im = value
                    pre, pim = probe[0, whole, cut], probe[1, whole, cut]
                    flat[s, whole, cut] = (pre * re - pim * im).astype(BF16)
                    flat[s, whole, 512 + 128 * j:640 + 128 * j] = (pre * im + pim * re).astype(BF16)

            rows = slice(b * RB, b * RB + RB)
            mid = product(flat[s, rows, :], rt[...]).astype(BF16)
            tall[s, rows, :] = mid[:, :N]
            tall[s, N + b * RB:N + b * RB + RB, :] = mid[:, N:]

    def middle():
        blocks = [(s, slice(256 * n, 256 * n + 256)) for s in range(SLOTS) for n in range(2)]

        def spread(i, r):
            s, cut = blocks[i]
            for start in (128 * r, N + 128 * r):
                wave[i % 2, start:start + 128, :] = product(lt[start:start + 128, :], tall[s, :, cut])

        def limit(i, r):
            s, cut = blocks[i]
            for m in range(128 * r, 128 * r + 128, 32):
                upper, lower = slice(m, m + 32), slice(N + m, N + m + 32)
                re, im = wave[i % 2, upper, :], wave[i % 2, lower, :]
                factor = amp[s, upper, cut] * lax.rsqrt(jnp.maximum(re * re + im * im, 0.0625))
                tall[s, upper, cut] = (re * factor).astype(BF16)
                tall[s, lower, cut] = (im * factor).astype(BF16)

        for r in range(4):
            spread(0, r)
        for i, (s, cut) in enumerate(blocks):
            for r in range(4):
                if i + 1 < len(blocks):
                    spread(i + 1, r)
                limit(i, r)
            for start in range(0, N, 256):
                rows = slice(start, start + 256)
                flat[s, rows, cut] = product(rt[rows, :], tall[s, :, cut]).astype(BF16)
                flat[s, rows, N + cut.start:N + cut.stop] = product(rt[N + start:N + start + 256, :], tall[s, :, cut]).astype(BF16)

    def rows_out(b):
        for s in range(SLOTS):
            back[...] = product(flat[s, b * RB:b * RB + RB, :], lt[...])

            for m in range(4):
                rows = rows_of(m * 32, 32)
                whole = rows_of(b * RB + m * 32, 32)
                last = [jnp.zeros((32, 128), F32)] * 2
                for j in range(5):
                    value = [jnp.zeros((32, 128), F32)] * 2
                    if j < 4:
                        cut = slice(128 * j, 128 * j + 128)
                        re, im = patch[s, 0, whole, cut], patch[s, 1, whole, cut]
                        pre, pim = probe[0, whole, cut], probe[1, whole, cut]
                        dre = (back[rows, cut] - (pre * re - pim * im)) * valid[s]
                        dim = (back[rows, 512 + 128 * j:640 + 128 * j] - (pre * im + pim * re)) * valid[s]
                        gre, gim = re * dre + im * dim, re * dim - im * dre
                        if s:
                            gre, gim = gre + probe_grad[0, whole, cut], gim + probe_grad[1, whole, cut]
                        probe_grad[0, whole, cut] = gre
                        probe_grad[1, whole, cut] = gim
                        value = [pre * dre + pim * dim, pre * dim - pim * dre]
                    for part in range(2):
                        turned = pltpu.roll(value[part], 64, 1) if j < 4 else value[part]
                        moved = jnp.where(lane < 64, last[part], turned)
                        last[part] = turned
                        parts[s][j + 1, part, rows, :] = jnp.where(odd[s], moved, value[part])

        def placed(t):
            spot = [jnp.clip(t - base[s], -1, 5) + 1 for s in range(SLOTS)]
            return parts[0][spot[0]] + parts[1][spot[1]]

        @pl.loop(0, 4)
        def _(k):
            for half in range(2):
                own[b, k, half] = placed(4 * k + 2 * links.c + half)
                theirs[b, k, half] = placed(4 * k + 2 * (1 - links.c) + half)

    for turn in range(ITERS):
        gather = Gather(links, tile, bands)
        gather.chain(0)
        gather.first(0)
        own_copy = pltpu.make_async_copy(tile, gather.at(0, gather.me), sems.at[4])
        own_copy.start()
        gather.relay(0)
        gather.first(1)
        if turn:
            p[5]()
        gather.second(0)
        gather.third(0)
        gather.relay(1)
        if turn == 0:
            for load in loads:
                load.wait()
        gather.first(2)
        gather.second(1)
        own_copy.wait()
        gather.third(1)
        gather.relay(2)
        if turn:
            p[6]()
        gather.first(3)
        if turn:
            p[7]()
        gather.done(0)
        rows_in(0)
        gather.second(2)
        gather.done(1)
        rows_in(1)
        gather.third(2)
        gather.relay(3)
        gather.done(2)
        rows_in(2)
        gather.second(3)
        gather.third(3)
        gather.done(3)
        rows_in(3)
        links.drain()
        middle()
        if turn:
            sum_links.drain()
            probe_links.drain()
        r = Reduce(sum_links, own, theirs, sibs, halves, wholes, chained)
        sums = ProbeSum(probe_links, probe_grad, probe, (from_sib, r1, s1, r2, r3), counts, counted, turn == 0)
        p = sums.steps()
        rows_out(3)
        r.zeroth(3)
        rows_out(2)
        r.zeroth(2)
        r.first(3)
        rows_out(1)
        rows_out(0)
        p[0]()
        r.zeroth(1)
        r.zeroth(0)
        r.second(3)
        r.first(2)
        if turn == 0:
            order = ((r.third, 3), p[1], (r.second, 2), (r.first, 1), (r.third, 2), (r.second, 1), p[2], (r.first, 0),
                     p[3], (r.third, 1), (r.second, 0), p[4], (r.third, 0))
        else:
            order = (p[1], (r.third, 3), (r.second, 2), (r.first, 1), p[2], (r.third, 2), p[3], (r.second, 1),
                     (r.first, 0), p[4], (r.third, 1), (r.second, 0), p[5], (r.third, 0), p[6])
        for step in order:
            if isinstance(step, tuple):
                total = step[0](step[1])
                if step == (r.third, 0):
                    tile[...] = tile[...] + 0.25 * total
            else:
                step()
    for t in range(2):
        field_out[:, :, 128 * t:128 * t + 128] = tile[t]
    mine = pltpu.make_async_copy(probe.at[links.c], probe_out.at[links.c], sems.at[5])
    mine.start()
    p[7]()
    other = pltpu.make_async_copy(probe.at[1 - links.c], probe_out.at[1 - links.c], sems.at[6])
    other.start()
    sum_links.drain()
    probe_links.drain()
    mine.wait()
    other.wait()


def hand_out(field, probe, field_out, probe_out, field_held, probe_held, sems):
    ways = [(field, field_held, field_out)]
    for k in range(8):
        part = (k // 4, pl.ds(128 * (k % 4), 128))
        ways.append((probe.at[part], probe_held.at[part], probe_out.at[part]))
    ins = [pltpu.make_async_copy(src, held, sems.at[0, k]) for k, (src, held, _) in enumerate(ways)]
    outs = [pltpu.make_async_copy(held, dst, sems.at[1, k]) for k, (_, held, dst) in enumerate(ways)]
    for copy in ins:
        copy.start()
    for arrived, onward in zip(ins, outs):
        arrived.wait()
        onward.start()
    for copy in outs:
        copy.wait()


def f32(*shape):
    return pltpu.VMEM(shape, F32)


def body(object_field, probe, scan_cols, amplitudes):
    left, right = (jnp.asarray(t) for t in tables())
    sends = GATHER_SENDS + REDUCE_SENDS + PROBE_SENDS
    anywhere = pl.BlockSpec(memory_space=pl.ANY)
    vmem = pl.BlockSpec(memory_space=pltpu.VMEM)
    field, probe = pl.pallas_call(
        kernel,
        name="reconstruct",
        out_shape=(jax.ShapeDtypeStruct((2, RB, 256), F32), jax.ShapeDtypeStruct((2, N, N), F32)),
        in_specs=[pl.BlockSpec(memory_space=pltpu.SMEM), vmem] + [anywhere] * 4,
        out_specs=(vmem, anywhere),
        scratch_shapes=[f32(16, 2, RB, 128)] * 4 + [
            f32(*TILE), f32(2, N, N), f32(2, N, N), pltpu.VMEM((1024, 1024), BF16), pltpu.VMEM((1024, 1024), BF16),
            f32(2, 2, N, N), pltpu.VMEM((2, N, 1024), BF16), pltpu.VMEM((2, 1024, N), BF16),
            f32(2, 1024, 256), f32(RB, 1024), f32(7, 2, RB, 128), f32(7, 2, RB, 128),
            f32(2, N, N), f32(4, 4, *TILE), f32(4, 4, *TILE), f32(4, 4, *TILE),
            f32(4, 2, 2, RB, 128), f32(4, 2, *TILE), f32(3, *TILE),
            f32(N, N), f32(2, 3, 128, 256), f32(2, 128, 256), f32(2, 3, 32, 256), f32(4, 2, 32, 256),
            f32(5, 8, 128), f32(4, 3, 8, 128),
            pltpu.SemaphoreType.DMA((sends,)), pltpu.SemaphoreType.DMA((sends,)), pltpu.SemaphoreType.DMA((7,)),
        ],
        compiler_params=pltpu.CompilerParams(vmem_limit_bytes=60 << 20, collective_id=1, has_side_effects=True),
    )(scan_cols, object_field, probe, amplitudes, left, right)
    return pl.pallas_call(
        hand_out,
        name="hand_out",
        out_shape=(jax.ShapeDtypeStruct((2, RB, 256), F32), jax.ShapeDtypeStruct((2, N, N), F32)),
        in_specs=[anywhere] * 2,
        out_specs=(anywhere, anywhere),
        scratch_shapes=[f32(2, RB, 256), f32(2, N, N), pltpu.SemaphoreType.DMA((2, 9))],
        compiler_params=pltpu.CompilerParams(vmem_limit_bytes=16 << 20),
    )(field, probe)


def solution(mesh):
    in_specs = (P(None, "obj", "pat"), P(), P(("obj", "pat")), P(("obj", "pat"), None, None))
    out_specs = (P(None, "obj", "pat"), P())
    return jax.shard_map(body, mesh=mesh, in_specs=in_specs, out_specs=out_specs, check_vma=False)
```
